128 devices in a mesh: dp: 8 (over x_lo, y), tensor: 16 (over x_hi, z, core).
Axes of the slice: x: 4 (x_hi: 2, x_lo: 2; x = x_hi * 2 + x_lo), y: 4, z: 4, core: 2. Of those that a mesh axis runs over, the one named last changes fastest.
Arguments:
- tokens: bfloat16 [1024, 16, 1024], P('tensor', 'dp'), may hold values from -6 to 6
- segments: int32 [16, 1024], P('dp'), may hold values from 0 to 3, as said below
- cotangent: bfloat16 [1024, 16, 1024], P('tensor', 'dp'), may hold values from -6 to 6
- w_qkv: bfloat16 [2, 3, 1024, 1024], P(None, None, 'dp', 'tensor'), may hold values from -0.1875 to 0.1875
- b_qv: bfloat16 [2, 2, 16, 64], P(None, None, 'tensor', 'dp'), may hold values from -3 to 3
- w_out: bfloat16 [2, 1024, 1024], P(None, 'tensor', 'dp'), may hold values from -1.5 to 1.5
- w_fc: bfloat16 [2, 1024, 4096], P(None, 'dp', 'tensor'), may hold values from -0.1875 to 0.1875
- b_fc: bfloat16 [2, 16, 256], P(None, 'tensor', 'dp'), may hold values from -3 to 3
- w_proj: bfloat16 [2, 4096, 1024], P(None, 'tensor', 'dp'), may hold values from -0.09375 to 0.09375
- norm_gains: bfloat16 [2, 2, 1024], P(None, None, 'dp'), may hold values from 0.25 to 1.75
- shifts: bfloat16 [2, 4, 1024], P(None, None, 'dp'), may hold values from -2 to 2
Outputs:
- out: bfloat16 [1024, 16, 1024], P('tensor', 'dp')
- g_tokens: float32 [1024, 16, 1024], P('tensor', 'dp')
- g_w_qkv: float32 [2, 3, 1024, 1024], P(None, None, 'dp', 'tensor')
- g_b_qv: float32 [2, 2, 16, 64], P(None, None, 'tensor', 'dp')
- g_w_out: float32 [2, 1024, 1024], P(None, 'tensor', 'dp')
- g_w_fc: float32 [2, 1024, 4096], P(None, 'dp', 'tensor')
- g_b_fc: float32 [2, 16, 256], P(None, 'tensor', 'dp')
- g_w_proj: float32 [2, 4096, 1024], P(None, 'tensor', 'dp')
- g_norm_gains: float32 [2, 2, 1024], P(None, None, 'dp')
- g_shifts: float32 [2, 4, 1024], P(None, None, 'dp')
The draws below stay inside these ranges and needn't reach their ends.
Inputs may be any that keep to these rules, and one draw needn't show every extreme that they name: `segments`: segment numbers never fall along a row; every document (a run of one number) holds at most 768 positions, and in every draw some row holds a document of exactly 768 positions.
All inputs are finite; a program needn't handle non-finite values.
Results may differ from the reference program's by a relative error of at most 0.023.
Values may be sent and summed in bfloat16 or wider, within the bound.
No kernel may reach another device: no remote copies, remote signals or barrier semaphores. Data moves between devices by JAX's collectives and lax.ppermute only.
A program may use at most 192 MiB of HBM per device.

```python
import jax
import jax.numpy as jnp
from jax import lax

D = 1024
HEADS = 16
HD = 64
FF = 4096
ROW_LEN = 1024
DOC_MOST = 768
LAYERS = 2
SEQS = 16


def draw_segments(key, part):
    key = jax.random.fold_in(key, 7)
    key_start, key_length, key_cut, key_pick = jax.random.split(key, 4)
    starts = jax.random.randint(key_start, (SEQS, 1), 0, ROW_LEN - DOC_MOST + 1)
    lengths = jax.random.randint(key_length, (SEQS, 1), DOC_MOST // 2, DOC_MOST + 1)
    chosen = jax.random.randint(key_pick, (), 0, SEQS)
    row_numbers = jnp.arange(SEQS, dtype=jnp.int32)[:, None]
    lengths = jnp.where(row_numbers == chosen, DOC_MOST, lengths)
    doc_ends = starts + lengths
    doc_cuts = doc_ends + jax.random.randint(key_cut, (SEQS, 1), 0, ROW_LEN + 1 - doc_ends)
    position = jnp.arange(ROW_LEN, dtype=jnp.int32)[None, :]
    first_mark = (position >= starts).astype(jnp.int32)
    second_mark = (position >= doc_ends).astype(jnp.int32)
    third_mark = (position >= doc_cuts).astype(jnp.int32)
    return first_mark + second_mark + third_mark


def steps_of(rng, dims, cuts, least, top_value):
    gain = 1.0
    for dim, shards_of in cuts:
        heights = jax.random.uniform(jax.random.fold_in(jax.random.fold_in(rng, 6), dim), (shards_of,), jnp.float32, least / len(cuts), top_value / len(cuts))
        gain = gain * jnp.repeat(jnp.exp(heights), dims[dim] // shards_of).reshape((-1,) + (1,) * (len(dims) - 1 - dim))
    return gain


def gaussian(key, extent, deviation, most, cuts=(), held_as=jnp.bfloat16):
    values = jax.random.normal(key, extent, jnp.float32) * deviation
    if len(cuts) > 0:
        values = steps_of(key, extent, cuts, -0.22, 0.18) * values
    return jnp.clip(values, min=-most, max=most).astype(held_as)


def setup_inputs(seed: int = 0) -> dict:
    key_of = jax.random.split(jax.random.key(seed), 12)
    tokens = gaussian(key_of[0], (ROW_LEN, SEQS, D), 1.0, 6.0, ((0, 16), (1, 8)))
    segments = draw_segments(jax.random.fold_in(key_of[11], 71), 0)
    cotangent = gaussian(key_of[2], (ROW_LEN, SEQS, D), 1.0, 6.0, ((0, 16), (1, 8)))
    w_qkv = gaussian(key_of[3], (LAYERS, 3, D, D), D ** -0.5, 0.1875, ((2, 8), (3, 16)))
    b_qv = gaussian(key_of[4], (LAYERS, 2, HEADS, HD), 0.5, 3.0, ((2, 16), (3, 8)))
    w_out = gaussian(key_of[5], (LAYERS, D, D), (D // 64) ** -0.5, 1.5, ((1, 16), (2, 8)))
    w_fc = gaussian(key_of[6], (LAYERS, D, FF), D ** -0.5, 0.1875, ((1, 8), (2, 16)))
    b_fc = gaussian(key_of[7], (LAYERS, HEADS, FF // HEADS), 0.5, 3.0, ((1, 16), (2, 8)))
    w_proj = gaussian(key_of[8], (LAYERS, FF, D), FF ** -0.5, 0.09375, ((1, 16), (2, 8)))
    norm_gains = jnp.clip(1.0 + 0.15 * jax.random.normal(key_of[9], (LAYERS, 2, D), jnp.float32), 0.25, 1.75).astype(jnp.bfloat16)
    shifts = gaussian(key_of[10], (LAYERS, 4, D), 0.3, 2.0, ((2, 8),))
    return dict(tokens=tokens, segments=segments, cotangent=cotangent, w_qkv=w_qkv, b_qv=b_qv, w_out=w_out, w_fc=w_fc, b_fc=b_fc, w_proj=w_proj, norm_gains=norm_gains, shifts=shifts)


@jax.custom_vjp
def low(v):
    return lax.optimization_barrier(v.astype(jnp.bfloat16)).astype(jnp.float32)

@jax.custom_vjp
def reduced_backward(v):
    return v

def low_keep(v):
    return (low(v), None)

def low_pass(kept, grad):
    return (grad,)

def back_keep(v):
    return (v, None)

def back_low(kept, grad):
    return (low(grad),)
low.defvjp(low_keep, low_pass)
reduced_backward.defvjp(back_keep, back_low)
EPS = 1e-05
PRECISE = lax.Precision.HIGHEST

def exact_dot(left, right):
    return jnp.dot(left, right, precision=PRECISE, preferred_element_type=jnp.float32)

def row_norm_values(values, gain_row, shift_row):
    center = values - lax.optimization_barrier(jnp.mean(values, axis=-1, keepdims=True))
    spread = lax.optimization_barrier(jnp.mean(center * center, axis=-1, keepdims=True))
    return center * lax.rsqrt(spread + EPS) * gain_row + shift_row

def attend_row(queries, keys_all, values_all, segment_row):
    length = queries.shape[1]
    positions = jnp.arange(length, dtype=jnp.int32)
    allowed = (segment_row[:, None] == segment_row[None, :]) & (positions[:, None] >= positions[None, :])
    scores = jnp.einsum('hqd,hkd->hqk', queries, keys_all, precision=PRECISE) * 0.125
    scores = reduced_backward(scores)
    scores = jnp.where(allowed[None], scores, -1e+30)
    highest = lax.optimization_barrier(jnp.max(scores, axis=-1, keepdims=True))
    raised = jnp.exp(scores - highest)
    probability = raised / lax.optimization_barrier(jnp.sum(raised, axis=-1, keepdims=True))
    return jnp.einsum('hqk,hkd->hqd', low(probability), values_all, precision=PRECISE)

def to_heads(values):
    return values.reshape(values.shape[0], HEADS, HD).transpose(1, 0, 2)

def block_row(params, row_values, segment_row):
    w_qkv, b_qv, w_out, w_fc, b_fc, w_proj, norm_gains, shifts = params
    residual = row_values
    length = row_values.shape[0]
    for layer_index in range(LAYERS):
        normed = low(row_norm_values(residual, norm_gains[layer_index, 0], shifts[layer_index, 0]))
        queries = low(reduced_backward(exact_dot(normed, w_qkv[layer_index, 0]) + b_qv[layer_index, 0].reshape(D)))
        keys_all = low(reduced_backward(exact_dot(normed, w_qkv[layer_index, 1])))
        values_all = low(reduced_backward(exact_dot(normed, w_qkv[layer_index, 2]) + b_qv[layer_index, 1].reshape(D)))
        mixed_heads = jax.checkpoint(attend_row)(to_heads(queries), to_heads(keys_all), to_heads(values_all), segment_row)
        mixed_heads = low(reduced_backward(mixed_heads.transpose(1, 0, 2).reshape(length, D)))
        residual = residual + reduced_backward(exact_dot(mixed_heads, w_out[layer_index]) + shifts[layer_index, 2])
        normed = low(row_norm_values(residual, norm_gains[layer_index, 1], shifts[layer_index, 1]))
        hidden_activation = reduced_backward(exact_dot(normed, w_fc[layer_index]) + b_fc[layer_index].reshape(FF))
        hidden_activation = low(jax.nn.gelu(hidden_activation, approximate=True))
        residual = residual + reduced_backward(exact_dot(hidden_activation, w_proj[layer_index]) + shifts[layer_index, 3])
    return residual

def reference(tokens, segments, cotangent, w_qkv, b_qv, w_out, w_fc, b_fc, w_proj, norm_gains, shifts):
    params = (w_qkv.astype(jnp.float32), b_qv.astype(jnp.float32), w_out.astype(jnp.float32), w_fc.astype(jnp.float32), b_fc.astype(jnp.float32), w_proj.astype(jnp.float32), norm_gains.astype(jnp.float32), shifts.astype(jnp.float32))
    inputs = tokens.astype(jnp.float32)
    seed_grads = cotangent.astype(jnp.float32)

    def one_row(totals, row_index):
        row_values = inputs[:, row_index]
        segment_row = segments[row_index]

        def forward(weights, values):
            return block_row(weights, values, segment_row)
        result, reverse_mapping = jax.vjp(forward, params, row_values)
        weight_grads, row_grad = reverse_mapping(seed_grads[:, row_index])
        totals = jax.tree.map(jnp.add, totals, weight_grads)
        return (totals, (result, row_grad))
    initial = jax.tree.map(jnp.zeros_like, params)
    totals, (results, row_grads) = lax.scan(one_row, initial, jnp.arange(SEQS, dtype=jnp.int32))
    output = results.transpose(1, 0, 2).astype(jnp.bfloat16)
    token_grads = row_grads.transpose(1, 0, 2)
    return (output, token_grads, totals[0], totals[1], totals[2], totals[3], totals[4], totals[5], totals[6], totals[7])
```

```python
import jax
import jax.numpy as jnp
from jax import lax
from jax.experimental import pallas as pl
from jax.experimental.pallas import tpu as pltpu
from jax.sharding import Mesh
from jax.sharding import PartitionSpec as P

EPS = 1e-05
F32 = jnp.float32
BF16 = jnp.bfloat16
X = ("xl", "xh")
HD = 64
NT = (((1,), (1,)), ((), ()))
TN = (((0,), (0,)), ((), ()))


def swap(value, axis, mask):
    count = lax.axis_size(axis)
    return lax.ppermute(value, axis, [(i, i ^ mask) for i in range(count)])


def gather_plane(block):
    m, r, c = block.shape
    one, three, two = (swap(block, "y", k) for k in (1, 3, 2))
    ys = jnp.stack([block, one, two, three], axis=1)
    low, both, high = (swap(ys, X, k) for k in (2, 3, 1))
    own = jnp.stack([ys, low, high, both], axis=1).reshape(m, 2, 8, r, c)
    other = swap(own, "c", 1)
    return jnp.concatenate([own, other], axis=1)


def scatter_plane(own, other, send_type):
    m, _, _, r, c = own.shape
    both = own + swap(other.astype(send_type), "c", 1).astype(F32)
    parts = both.reshape(m, 4, 4, r, c)
    total = parts[:, 0]
    for k, mask in ((1, 2), (3, 3), (2, 1)):
        total = total + swap(parts[:, k].astype(send_type), X, mask).astype(F32)
    final = total[:, 0]
    for k in (1, 3, 2):
        final = final + swap(total[:, k].astype(send_type), "y", k).astype(F32)
    return final


def gather_tokens(own):
    t, n = own.shape
    got = {0: own}
    for k in (1, 3, 2):
        got[k] = swap(own, "z", k)
    return jnp.stack([got[k].reshape(2, t // 2, n) for k in range(4)], axis=1).reshape(4 * t, n)


def scatter_tokens(partial):
    t, n = partial.shape
    parts = partial.reshape(2, 4, t // 8, n)
    total = parts[:, 0].reshape(t // 4, n)
    for k in (1, 3, 2):
        total = total + swap(parts[:, k].reshape(t // 4, n).astype(BF16), "z", k).astype(F32)
    return total


def relative(value, d_own):
    for bit in (1, 2, 4):
        half = 128 * bit
        shape = value.shape
        cut = value.reshape(*shape[:-1], shape[-1] // (2 * half), 2, half)
        turned = jnp.concatenate([cut[..., 1:, :], cut[..., :1, :]], axis=-2).reshape(shape)
        value = jnp.where((d_own & bit) != 0, turned, value)
    return value


def norm_parts(values):
    center = values - jnp.mean(values, axis=-1, keepdims=True)
    spread = jnp.mean(center * center, axis=-1, keepdims=True)
    rstd = lax.rsqrt(spread + EPS)
    return center * rstd, rstd


def norm_rows(values, gain, shift):
    return (norm_parts(values)[0] * gain + shift).astype(BF16)


def norm_back(values, gain, grad):
    xhat, rstd = norm_parts(values)
    dxhat = grad * gain
    into = dxhat - jnp.mean(dxhat, axis=-1, keepdims=True)
    into = (into - xhat * jnp.mean(dxhat * xhat, axis=-1, keepdims=True)) * rstd
    return into, jnp.sum(grad * xhat, axis=0), jnp.sum(grad, axis=0)


def gelu_and_slope(pre):
    a, b = 0.7978845608028654, 0.044715
    square = pre * pre
    th = jnp.tanh(a * pre * (1.0 + b * square))
    value = 0.5 * pre * (1.0 + th)
    slope = 0.5 * (1.0 + th) + 0.5 * pre * (1.0 - th * th) * a * (1.0 + 3.0 * b * square)
    return value, slope


def head_keys(kv_ref, par_ref):
    half = kv_ref.shape[1] // 2
    return jnp.concatenate(
        [kv_ref[0, :half], par_ref[0, :half], kv_ref[0, half:], par_ref[0, half:]], axis=0
    )


def attend_kernel(kv_ref, par_ref, q_ref, bias_ref, mixed_ref, lse_ref):
    kv = head_keys(kv_ref, par_ref)
    count = q_ref.shape[1]
    half = count // 2
    for part in range(2):
        rows = slice(part * half, (part + 1) * half)
        seen = count * (part + 1)
        keys = kv[:seen]
        scores = lax.dot_general(q_ref[0, rows], keys, NT, preferred_element_type=F32)
        scores = scores + bias_ref[rows, :seen]
        highest = jnp.max(scores, axis=1, keepdims=True)
        raised = jnp.exp(scores - highest)
        totals = jnp.sum(raised, axis=1, keepdims=True)
        probs = (raised * (1.0 / totals)).astype(BF16)
        mixed = jnp.dot(probs, keys, preferred_element_type=F32)
        lane = lax.broadcasted_iota(jnp.int32, mixed.shape, 1)
        mixed_ref[0, rows] = jnp.where(lane >= HD, mixed, 0.0).astype(BF16)
        lse_ref[0, rows] = highest + jnp.log(totals)


def attend_back_kernel(
    kv_ref, par_ref, q_ref, bias_ref, lse_ref, dm_ref, dq_ref, own_ref, other_ref
):
    kv = head_keys(kv_ref, par_ref)
    count = q_ref.shape[1]
    half = count // 2
    sums = []
    for part in range(2):
        rows = slice(part * half, (part + 1) * half)
        seen = count * (part + 1)
        keys = kv[:seen]
        queries = q_ref[0, rows]
        grad = dm_ref[0, rows]
        scores = lax.dot_general(queries, keys, NT, preferred_element_type=F32)
        probs = jnp.exp(scores + bias_ref[rows, :seen] - lse_ref[0, rows])
        dprobs = lax.dot_general(grad, keys, NT, preferred_element_type=F32)
        inner = jnp.sum(probs * dprobs, axis=1, keepdims=True)
        dscores = (probs * (dprobs - inner)).astype(BF16)
        low = probs.astype(BF16)
        dq = jnp.dot(dscores, keys, preferred_element_type=F32) * 0.125
        lane = lax.broadcasted_iota(jnp.int32, dq.shape, 1)
        dq_ref[0, rows] = jnp.where(lane < HD, dq, 0.0).astype(BF16)
        sums.append(
            lax.dot_general(dscores, queries, TN, preferred_element_type=F32)
            + lax.dot_general(low, grad, TN, preferred_element_type=F32)
        )
    low_keys = sums[0] + sums[1][:count]
    own_ref[0, :half] = low_keys[:half]
    other_ref[0, :half] = low_keys[half:].astype(BF16)
    own_ref[0, half:] = sums[1][count : count + half]
    other_ref[0, half:] = sums[1][count + half :].astype(BF16)


def head_spec(rows, index, lanes=128, column=0):
    return pl.BlockSpec((1, rows, lanes), lambda t: (index(t), 0, column))


def same(t):
    return t


def across(t):
    return lax.rem(t + 2, 4)


def attend(qkvo, par, bias):
    heads, count, _ = qkvo.shape
    area = heads * count * 2 * count
    return pl.pallas_call(
        attend_kernel,
        grid=(heads,),
        in_specs=[
            head_spec(count, same),
            head_spec(count, across),
            head_spec(count, same, column=1),
            pl.BlockSpec(bias.shape, lambda t: (0, 0)),
        ],
        out_specs=[head_spec(count, same), head_spec(count, same, lanes=1)],
        out_shape=[
            jax.ShapeDtypeStruct((heads, count, 128), BF16),
            jax.ShapeDtypeStruct((heads, count, 1), F32),
        ],
        compiler_params=pltpu.CompilerParams(vmem_limit_bytes=40 << 20),
        cost_estimate=pl.CostEstimate(
            flops=area * 512, bytes_accessed=6 << 20, transcendentals=area
        ),
    )(qkvo, par, qkvo, bias)


def attend_back(qkvo, par, bias, lse, grad):
    heads, count, _ = qkvo.shape
    area = heads * count * 2 * count
    return pl.pallas_call(
        attend_back_kernel,
        grid=(heads,),
        in_specs=[
            head_spec(count, same),
            head_spec(count, across),
            head_spec(count, same, column=1),
            pl.BlockSpec(bias.shape, lambda t: (0, 0)),
            head_spec(count, same, lanes=1),
            head_spec(count, same),
        ],
        out_specs=[head_spec(count, same)] * 3,
        out_shape=[
            jax.ShapeDtypeStruct((heads, count, 128), BF16),
            jax.ShapeDtypeStruct((heads, count, 128), F32),
            jax.ShapeDtypeStruct((heads, count, 128), BF16),
        ],
        compiler_params=pltpu.CompilerParams(vmem_limit_bytes=40 << 20),
        cost_estimate=pl.CostEstimate(
            flops=area * 1280, bytes_accessed=8 << 20, transcendentals=area
        ),
    )(qkvo, par, qkvo, bias, lse, grad)


def into_blocks(rows, weight):
    return jnp.einsum("nd,tdk->tnk", rows, weight, preferred_element_type=F32)


def out_of_blocks(blocks, weight):
    return jnp.einsum("tnk,tdk->nd", blocks, weight, preferred_element_type=F32)


def weight_grad(rows, blocks):
    return jnp.einsum("nd,tnk->tdk", rows, blocks, preferred_element_type=F32)


def on_device(
    tokens, segments, cotangent, w_qkv, b_qv, w_out, w_fc, b_fc, w_proj, norm_gains, shifts
):
    layers = w_qkv.shape[0]
    xl, y, xh, z, core = (lax.axis_index(a) for a in ("xl", "y", "xh", "z", "c"))
    d_own = xl * 4 + y
    first = xh == 0
    block, _, width = tokens.shape
    to_own = jnp.arange(8, dtype=jnp.int32) ^ d_own

    def by_row(value):
        kept = jnp.where(first, value[:, 0], value[:, 1])
        sent = jnp.where(first, value[:, 1], value[:, 0])
        got = swap(sent, "xh", 1)
        both = jnp.concatenate(
            [jnp.where(first, kept, got), jnp.where(first, got, kept)], axis=0
        )
        return relative(both, d_own)

    def by_position(value):
        value = relative(value, d_own)
        lower, upper = value[:block], value[block:]
        kept = jnp.where(first, lower, upper)
        got = swap(jnp.where(first, upper, lower).astype(BF16), "xh", 1).astype(value.dtype)
        return jnp.stack([jnp.where(first, kept, got), jnp.where(first, got, kept)], axis=1)

    attn_blocks = jnp.concatenate(
        [w_qkv[:, 1], w_qkv[:, 2], w_qkv[:, 0], jnp.swapaxes(w_out, 1, 2)], axis=2
    )
    proj_blocks = jnp.swapaxes(w_proj, 1, 2)
    small = jnp.concatenate(
        [
            jnp.pad(
                jnp.concatenate([b_qv.reshape(layers, 1, -1), b_fc.reshape(layers, 1, -1)], axis=2),
                ((0, 0), (0, 0), (0, 128 - 48)),
            ),
            norm_gains,
            shifts,
            jnp.zeros((layers, 1, 128), BF16),
        ],
        axis=1,
    )
    small_all = gather_plane(small)
    attn_w, fc_w, proj_w = [], [], []
    for i in range(layers):
        for store, source in ((attn_w, attn_blocks), (fc_w, w_fc), (proj_w, proj_blocks)):
            store.append(gather_plane(source[i][None]).reshape(4, width, 256))

    gains = jnp.swapaxes(small_all[:, 0, :, 1:3], 1, 2).reshape(layers, 2, width).astype(F32)
    shift = jnp.swapaxes(small_all[:, 0, :, 3:7], 1, 2).reshape(layers, 4, width).astype(F32)
    biases = jnp.take(small_all[:, :, :, 0, :48], to_own, axis=2).astype(F32)
    q_bias = biases[..., :8].reshape(layers, 4, HD)
    v_bias = biases[..., 8:16].reshape(layers, 4, HD)
    fc_bias = biases[..., 16:].reshape(layers, 4, 256)
    none = jnp.zeros_like(q_bias)
    qkvo_bias = jnp.concatenate([none, v_bias, q_bias, none], axis=2)
    column = jnp.arange(256)
    scale = jnp.where(column < 2 * HD, 1.0, jnp.where(column < 3 * HD, 0.125, 0.0)).astype(F32)

    seg_row = jnp.where(first, segments[0], segments[1])
    position = jnp.arange(seg_row.shape[0], dtype=jnp.int32)

    def at_core(value, which):
        cut = value.reshape(2, 4, 2, block)
        cut = jnp.where(which == 0, cut[:, :, 0], cut[:, :, 1])
        for bit in (1, 2):
            cut = jnp.where(
                (z & bit) != 0, cut[:, jnp.array([k ^ bit for k in range(4)])], cut
            )
        return cut.reshape(2, 4 * block)

    own_pos, own_seg = at_core(position, core), at_core(seg_row, core)
    par_pos, par_seg = at_core(position, 1 - core), at_core(seg_row, 1 - core)
    q_pos, q_seg = own_pos.reshape(-1, 1), own_seg.reshape(-1, 1)
    k_pos = jnp.concatenate([own_pos, par_pos], axis=1).reshape(1, -1)
    k_seg = jnp.concatenate([own_seg, par_seg], axis=1).reshape(1, -1)
    bias = jnp.where((q_seg == k_seg) & (q_pos >= k_pos), 0.0, -1e30).astype(F32)

    own_tokens = by_row(tokens)
    all_tokens = gather_tokens(own_tokens)
    residual = own_tokens.astype(F32)
    own_cotangent = by_row(cotangent)
    all_cotangent = gather_tokens(own_cotangent)

    kept = []
    for i in range(layers):
        attn_input = residual
        if i == 0:
            attn_rows = norm_rows(all_tokens.astype(F32), gains[i, 0], shift[i, 0])
        else:
            attn_rows = gather_tokens(norm_rows(residual, gains[i, 0], shift[i, 0]))
        qkvo = (
            (into_blocks(attn_rows, attn_w[i]) + qkvo_bias[i][:, None, :]) * scale
        ).astype(BF16)
        par = swap(qkvo[:, :, :128], "c", 1)
        mixed, lse = attend(qkvo, par, bias)
        attn_out = scatter_tokens(out_of_blocks(mixed, attn_w[i][:, :, 128:]))
        residual = residual + attn_out + shift[i, 2]
        mlp_input = residual
        mlp_rows = gather_tokens(norm_rows(residual, gains[i, 1], shift[i, 1]))
        pre = into_blocks(mlp_rows, fc_w[i]) + fc_bias[i][:, None, :]
        hidden = gelu_and_slope(pre)[0].astype(BF16)
        mlp_out = scatter_tokens(out_of_blocks(hidden, proj_w[i]))
        residual = residual + mlp_out + shift[i, 3]
        kept.append(
            (attn_input, attn_rows, qkvo, par, mixed, lse, mlp_input, mlp_rows, pre, hidden)
        )
    output = by_position(residual.astype(BF16))

    gradient = own_cotangent.astype(F32)
    big, gain_grads, shift_grads, bias_grads = [], [], [], []
    for i in reversed(range(layers)):
        attn_input, attn_rows, qkvo, par, mixed, lse, mlp_input, mlp_rows, pre, hidden = kept[i]
        low = gradient.astype(BF16)
        shift_mlp = jnp.sum(low.astype(F32), axis=0)
        grad_rows = all_cotangent if i == layers - 1 else gather_tokens(low)
        d_hidden = into_blocks(grad_rows, proj_w[i])
        d_pre = (d_hidden * gelu_and_slope(pre)[1]).astype(BF16)
        d_normed = scatter_tokens(out_of_blocks(d_pre, fc_w[i]))
        proj_grad = weight_grad(grad_rows, hidden)
        fc_grad = weight_grad(mlp_rows, d_pre)
        fc_bias_grad = jnp.sum(d_pre.astype(F32), axis=1)
        into, gain_mlp, shift_norm_mlp = norm_back(mlp_input, gains[i, 1], d_normed)
        gradient = gradient + into
        low = gradient.astype(BF16)
        shift_attn = jnp.sum(low.astype(F32), axis=0)
        grad_rows = gather_tokens(low)
        d_mixed = into_blocks(grad_rows, attn_w[i][:, :, 128:])
        d_mixed = jnp.where(jnp.arange(128) >= HD, d_mixed, 0.0).astype(BF16)
        dq, own_dkv, other_dkv = attend_back(qkvo, par, bias, lse, d_mixed)
        from_core = jnp.concatenate([(got := swap(other_dkv, "c", 1))[2:], got[:2]], axis=0)
        dkv = (own_dkv + from_core.astype(F32)).astype(BF16)
        d_qkvo = jnp.concatenate([dkv, dq], axis=2)
        d_normed = scatter_tokens(out_of_blocks(d_qkvo, attn_w[i]))
        mixed_wide = jnp.concatenate([jnp.zeros_like(mixed), mixed], axis=2)
        attn_grad = weight_grad(attn_rows, d_qkvo) + weight_grad(grad_rows, mixed_wide)
        qkvo_bias_grad = jnp.sum(d_qkvo.astype(F32), axis=1)
        into, gain_attn, shift_norm_attn = norm_back(attn_input, gains[i, 0], d_normed)
        gradient = gradient + into
        gain_grads.append(jnp.stack([gain_attn, gain_mlp]))
        shift_grads.append(jnp.stack([shift_norm_attn, shift_norm_mlp, shift_attn, shift_mlp]))
        bias_grads.append(
            jnp.concatenate(
                [
                    qkvo_bias_grad[:, 128:192].reshape(4, 8, 8),
                    qkvo_bias_grad[:, 64:128].reshape(4, 8, 8),
                    fc_bias_grad.reshape(4, 8, 32),
                ],
                axis=2,
            )
        )
        shards = []
        for grad in (attn_grad, fc_grad, proj_grad):
            cut = grad.reshape(1, 4, 8, 128, 256)
            shards.append(scatter_plane(cut[:, :2], cut[:, 2:], BF16)[0])
        big.append(shards)
    g_tokens = by_position(gradient)

    big, gain_grads, shift_grads, bias_grads = (
        a[::-1] for a in (big, gain_grads, shift_grads, bias_grads)
    )
    vectors = jnp.concatenate([jnp.stack(gain_grads), jnp.stack(shift_grads)], axis=1)
    vectors = jnp.swapaxes(vectors.reshape(layers, 6, 8, 128), 1, 2)
    vectors = jnp.broadcast_to(vectors[:, None], (layers, 4, 8, 6, 128))
    bias_rows = jnp.take(jnp.stack(bias_grads), to_own, axis=2)
    bias_rows = jnp.pad(bias_rows, ((0, 0), (0, 0), (0, 0), (0, 80)))[:, :, :, None]
    packed = jnp.concatenate([bias_rows, vectors, jnp.zeros_like(bias_rows)], axis=3)
    mine = scatter_plane(packed[:, :2], packed[:, 2:], F32)
    over_z = mine
    for k in (1, 3, 2):
        over_z = over_z + swap(mine, "z", k)
    g_b_qv = mine[:, 0, :16].reshape(layers, 2, 1, 8)
    g_b_fc = mine[:, 0, 16:48].reshape(layers, 1, 32)
    g_norm_gains = over_z[:, 1:3]
    g_shifts = over_z[:, 3:7]
    attn_all = jnp.stack([b[0] for b in big])
    g_w_qkv = jnp.stack(
        [attn_all[:, :, 128:192], attn_all[:, :, :64], attn_all[:, :, 64:128]], axis=1
    )
    g_w_out = jnp.swapaxes(attn_all[:, :, 192:], 1, 2)
    g_w_fc = jnp.stack([b[1] for b in big])
    g_w_proj = jnp.stack([jnp.swapaxes(b[2], 0, 1) for b in big])
    return (
        output,
        g_tokens,
        g_w_qkv,
        g_b_qv,
        g_w_out,
        g_w_fc,
        g_b_fc,
        g_w_proj,
        g_norm_gains,
        g_shifts,
    )


def solution(mesh):
    split = Mesh(mesh.devices.reshape(2, 4, 2, 4, 2), ("xl", "y", "xh", "z", "c"))
    dp, tensor = ("xl", "y"), ("xh", "z", "c")
    rows = P(tensor, dp, None)
    weights = (
        P(None, None, dp, tensor),
        P(None, None, tensor, dp),
        P(None, tensor, dp),
        P(None, dp, tensor),
        P(None, tensor, dp),
        P(None, tensor, dp),
        P(None, None, dp),
        P(None, None, dp),
    )
    return jax.shard_map(
        on_device,
        mesh=split,
        in_specs=(rows, P(dp, None), rows, *weights),
        out_specs=(rows, rows, *weights),
        check_vma=False,
    )
```

```python
import functools

import jax
import jax.numpy as jnp
from jax import lax
from jax.experimental import pallas as pl
from jax.experimental.pallas import tpu as pltpu
from jax.sharding import Mesh
from jax.sharding import PartitionSpec as P

EPS = 1e-05
F32 = jnp.float32
BF16 = jnp.bfloat16
X = ("xl", "xh")
PLANE = ("xl", "y", "xh", "c")
HD = 64
OWN = 128
SEEN = 512
WIDTH = 1024
VMEM = 20 << 20
NT = (((1,), (1,)), ((), ()))
TN = (((0,), (0,)), ((), ()))


def swap(value, axis, mask):
    count = lax.axis_size(axis)
    return lax.ppermute(value, axis, [(i, i ^ mask) for i in range(count)])


def over_z(value):
    two, one, three = (swap(value, "z", k) for k in (2, 1, 3))
    return value, one, two, three


def exchanged(parts):
    two, one, three = (swap(parts[k], "z", k) for k in (2, 1, 3))
    return parts[0], one, two, three


def tied(*values):
    return lax.optimization_barrier(values)


def swaps_x(parts):
    return [swap(part, X, mask) for part, mask in zip(parts, (2, 1, 3))]


def swaps_y(parts):
    one, three, two = (swap(parts[k - 1], "y", k) for k in (1, 3, 2))
    return one, two, three


def call(kernel, name, grid, ins, outs, scratch=(), flops=0, exps=0, prefetch=None):
    arrays = [a for a, _, _ in ins]
    in_specs = [pl.BlockSpec(block, index) for _, block, index in ins]
    out_specs = [pl.BlockSpec(block, index) for _, _, block, index in outs]
    shapes = [jax.ShapeDtypeStruct(shape, kind) for shape, kind, _, _ in outs]
    moved = sum(a.size * a.dtype.itemsize for a in arrays)
    moved += sum(s.size * s.dtype.itemsize for s in shapes)
    keys = dict(
        out_shape=shapes,
        name=name,
        compiler_params=pltpu.CompilerParams(vmem_limit_bytes=VMEM),
        cost_estimate=pl.CostEstimate(flops=flops, bytes_accessed=moved, transcendentals=exps),
    )
    if prefetch is None:
        return pl.pallas_call(
            kernel,
            grid=grid,
            in_specs=in_specs,
            out_specs=out_specs,
            scratch_shapes=list(scratch),
            **keys,
        )(*arrays)
    spec = pltpu.PrefetchScalarGridSpec(
        num_scalar_prefetch=1,
        grid=grid,
        in_specs=in_specs,
        out_specs=out_specs,
        scratch_shapes=list(scratch),
    )
    return pl.pallas_call(kernel, grid_spec=spec, **keys)(prefetch, *arrays)


def whole(array):
    return (array, array.shape, lambda *_: (0,) * array.ndim)


def weight_of(store, lanes=256, column=0):
    array, row = store
    return (array, (8, 4, 128, lanes), lambda *_: (0, 0, row, column))


def out_whole(shape, kind):
    return (shape, kind, shape, lambda *_: (0,) * len(shape))


def out_parts():
    return [out_whole((OWN, WIDTH), BF16)] * 4


def matrix(ref, t):
    return ref[:, t].reshape(8 * ref.shape[2], ref.shape[3])


def turned_product(blocks, ref, emit):
    left = jnp.concatenate(blocks, axis=1)
    for d in range(4):
        pieces = [
            ref[2 * d : 2 * d + 2, t].reshape(2 * ref.shape[2], ref.shape[3]) for t in range(4)
        ]
        right = jnp.concatenate(pieces, axis=1)
        value = lax.dot_general(left, right, NT, preferred_element_type=F32)
        emit(slice(d * 256, (d + 1) * 256), value)


def into_parts(parts):
    def emit(columns, value):
        for k, part in enumerate(parts):
            part[:, columns] = value[k * OWN : (k + 1) * OWN].astype(BF16)

    return emit


def xhat_of(values):
    center = values - jnp.mean(values, axis=-1, keepdims=True)
    rstd = lax.rsqrt(jnp.mean(center * center, axis=-1, keepdims=True) + EPS)
    return center * rstd, rstd


def fill_rows(sources, rows_ref, gain_ref=None, shift_ref=None):
    for k, source in enumerate(sources):
        value = source[...]
        if gain_ref is not None:
            value = xhat_of(value.astype(F32))[0] * gain_ref[0:1] + shift_ref[0:1]
            value = value.astype(BF16)
        rows_ref[k * OWN : (k + 1) * OWN] = value


def project_kernel(normalize, *refs):
    sources, refs = refs[:4], refs[4:]
    gain_ref, shift_ref = None, None
    if normalize:
        (gain_ref, shift_ref), refs = refs[:2], refs[2:]
    w_ref, bias_ref, scale_ref, rows_ref, q_ref, kv_ref = refs
    fill_rows(sources, rows_ref, gain_ref, shift_ref)
    for t in range(4):
        value = jnp.dot(rows_ref[...], matrix(w_ref, t), preferred_element_type=F32)
        value = ((value + bias_ref[t, 0:1]) * scale_ref[0:1]).astype(BF16)
        q_ref[t] = value[:, 128:]
        kv_ref[t] = value[:, :128]


def project(sources, norm, store, bias, scale):
    ins = [whole(s) for s in sources] + [whole(n) for n in norm]
    ins += [weight_of(store), whole(bias), whole(scale)]
    return call(
        functools.partial(project_kernel, len(norm) > 0),
        "project",
        (1,),
        ins,
        [out_whole((SEEN, WIDTH), BF16)] + [out_whole((4, SEEN, 128), BF16)] * 2,
        flops=2 * SEEN * WIDTH * 1024,
    )


def half_rows(value, part):
    step = OWN // 2
    return jnp.concatenate(
        [value[k * OWN + part * step : k * OWN + (part + 1) * step] for k in range(4)], axis=0
    )


def store_half(ref, t, part, value):
    step = OWN // 2
    for k in range(4):
        ref[t, k * OWN + part * step : k * OWN + (part + 1) * step] = value[
            k * step : (k + 1) * step
        ]


def head_keys(kv, par):
    return jnp.concatenate(
        [half_rows(kv, 0), half_rows(par, 0), half_rows(kv, 1), half_rows(par, 1)], axis=0
    )


def attend_kernel(kv_ref, par_ref, q_ref, bias_ref, w_ref, mixed_ref, lse_ref, *parts):
    half = SEEN // 2
    for t in range(4):
        kv = head_keys(kv_ref[t], par_ref[t])
        queries = q_ref[t]
        for part in range(2):
            rows = slice(part * half, (part + 1) * half)
            seen = SEEN * (part + 1)
            keys = kv[:seen]
            scores = lax.dot_general(
                half_rows(queries, part), keys, NT, preferred_element_type=F32
            )
            scores = scores + bias_ref[rows, :seen]
            highest = jnp.max(scores, axis=1, keepdims=True)
            raised = jnp.exp(scores - highest)
            totals = jnp.sum(raised, axis=1, keepdims=True)
            probs = (raised * (1.0 / totals)).astype(BF16)
            mixed = jnp.dot(probs, keys, preferred_element_type=F32)
            lane = lax.broadcasted_iota(jnp.int32, mixed.shape, 1)
            store_half(mixed_ref, t, part, jnp.where(lane >= HD, mixed, 0.0).astype(BF16))
            lse_ref[t, rows] = highest + jnp.log(totals)
    turned_product([mixed_ref[t] for t in range(4)], w_ref, into_parts(parts))


AREA = 4 * SEEN * 768


def attend(queries, kv, par, bias, store):
    return call(
        attend_kernel,
        "attend",
        (1,),
        [whole(kv), whole(par), whole(queries), whole(bias), weight_of(store, 128, 1)],
        [
            out_whole((4, SEEN, 128), BF16),
            out_whole((4, SEEN, 1), F32),
            *out_parts(),
        ],
        flops=AREA * 3700,
        exps=AREA,
    )


def attend_back_kernel(g0, g1, g2, g3, w_ref, kv_ref, par_ref, q_ref, bias_ref, lse_ref, *outs):
    rows_ref, dq_ref, own_ref, other_ref = outs
    fill_rows((g0, g1, g2, g3), rows_ref)
    half = SEEN // 2
    for t in range(4):
        d_mixed = jnp.dot(rows_ref[...], matrix(w_ref, t), preferred_element_type=F32)
        lane = lax.broadcasted_iota(jnp.int32, d_mixed.shape, 1)
        d_mixed = jnp.where(lane >= HD, d_mixed, 0.0).astype(BF16)
        kv = head_keys(kv_ref[t], par_ref[t])
        all_queries = q_ref[t]
        sums = []
        for part in range(2):
            rows = slice(part * half, (part + 1) * half)
            seen = SEEN * (part + 1)
            keys = kv[:seen]
            queries = half_rows(all_queries, part)
            grad = half_rows(d_mixed, part)
            scores = lax.dot_general(queries, keys, NT, preferred_element_type=F32)
            probs = jnp.exp(scores + bias_ref[rows, :seen] - lse_ref[t, rows])
            dprobs = lax.dot_general(grad, keys, NT, preferred_element_type=F32)
            inner = jnp.sum(probs * dprobs, axis=1, keepdims=True)
            dscores = (probs * (dprobs - inner)).astype(BF16)
            low = probs.astype(BF16)
            dq = jnp.dot(dscores, keys, preferred_element_type=F32) * 0.125
            lane = lax.broadcasted_iota(jnp.int32, dq.shape, 1)
            store_half(dq_ref, t, part, jnp.where(lane < HD, dq, 0.0).astype(BF16))
            sums.append(
                lax.dot_general(dscores, queries, TN, preferred_element_type=F32)
                + lax.dot_general(low, grad, TN, preferred_element_type=F32)
            )
        lower = sums[0] + sums[1][:SEEN]
        upper = sums[1][SEEN:]
        for part, value in enumerate((lower, upper)):
            store_half(own_ref, t, part, value[:half])
            store_half(other_ref, t, part, value[half:].astype(BF16))


def attend_back(sources, store, queries, kv, par, bias, lse):
    return call(
        attend_back_kernel,
        "attend_back",
        (1,),
        [whole(s) for s in sources]
        + [weight_of(store, 128, 1)]
        + [whole(a) for a in (kv, par, queries, bias, lse)],
        [
            out_whole((SEEN, WIDTH), BF16),
            out_whole((4, SEEN, 128), BF16),
            out_whole((4, SEEN, 128), F32),
            out_whole((4, SEEN, 128), BF16),
        ],
        flops=AREA * 6200,
        exps=AREA,
    )


def rejoin_kernel(norm_sums, own_ref, got_ref, dq_ref, w_ref, *refs):
    tokens, refs = refs[: 4 * norm_sums], refs[4 * norm_sums :]
    d_ref, sum_ref, p0, p1, p2, p3, *rest = refs
    for t in range(4):
        dkv = (own_ref[t] + got_ref[t].astype(F32)).astype(BF16)
        value = jnp.concatenate([dkv, dq_ref[t]], axis=1)
        d_ref[t] = value
        sums = jnp.sum(value.astype(F32), axis=0, keepdims=True)
        sum_ref[t] = jnp.broadcast_to(sums, sum_ref.shape[1:])
    blocks = [d_ref[t] for t in range(4)]
    emit = into_parts((p0, p1, p2, p3))
    if not norm_sums:
        turned_product(blocks, w_ref, emit)
        return
    norm_ref, xhat_ref = rest
    for k in range(4):
        xhat_ref[k * OWN : (k + 1) * OWN] = xhat_of(tokens[k][...].astype(F32))[0]
    norm_ref[...] = jnp.zeros_like(norm_ref)

    def emit_sums(columns, value):
        emit(columns, value)
        norm_ref[0:1, columns] = jnp.sum(value * xhat_ref[:, columns], axis=0, keepdims=True)
        norm_ref[1:2, columns] = jnp.sum(value, axis=0, keepdims=True)

    turned_product(blocks, w_ref, emit_sums)


def rejoin(own, got, dq, store, tokens=()):
    outs = [out_whole((4, SEEN, 256), BF16), out_whole((4, 8, 256), F32), *out_parts()]
    scratch = []
    if tokens:
        outs.append(out_whole((8, WIDTH), F32))
        scratch.append(pltpu.VMEM((SEEN, WIDTH), F32))
    return call(
        functools.partial(rejoin_kernel, len(tokens) > 0),
        "rejoin",
        (1,),
        [whole(own), whole(got), whole(dq), weight_of(store)] + [whole(t) for t in tokens],
        outs,
        scratch,
        flops=2 * SEEN * WIDTH * 1024,
    )


def gelu_parts(pre):
    a, b = 0.7978845608028654, 0.044715
    square = pre * pre
    return square, jnp.tanh(a * pre * (1.0 + b * square)), a, b


def feed_kernel(x0, x1, x2, x3, fc_ref, proj_ref, bias_ref, rows_ref, pre_ref, hid_ref, *parts):
    fill_rows((x0, x1, x2, x3), rows_ref)
    blocks = []
    for t in range(4):
        pre = jnp.dot(rows_ref[...], matrix(fc_ref, t), preferred_element_type=F32)
        pre = pre + bias_ref[t, 0:1]
        pre_ref[t] = pre
        _, th, _, _ = gelu_parts(pre)
        hidden = (0.5 * pre * (1.0 + th)).astype(BF16)
        hid_ref[t] = hidden
        blocks.append(hidden)
    turned_product(blocks, proj_ref, into_parts(parts))


def feed(sources, fc, proj, bias):
    return call(
        feed_kernel,
        "feed",
        (1,),
        [whole(s) for s in sources] + [weight_of(fc), weight_of(proj), whole(bias)],
        [
            out_whole((SEEN, WIDTH), BF16),
            out_whole((4, SEEN, 256), F32),
            out_whole((4, SEEN, 256), BF16),
            *out_parts(),
        ],
        flops=8 * SEEN * WIDTH * 1024,
        exps=SEEN * 1024,
    )


def feed_back_kernel(g0, g1, g2, g3, fc_ref, proj_ref, pre_ref, rows_ref, d_ref, sum_ref, *parts):
    fill_rows((g0, g1, g2, g3), rows_ref)
    blocks = []
    for t in range(4):
        d_hidden = jnp.dot(rows_ref[...], matrix(proj_ref, t), preferred_element_type=F32)
        pre = pre_ref[t]
        square, th, a, b = gelu_parts(pre)
        slope = 0.5 * (1.0 + th) + 0.5 * pre * (1.0 - th * th) * a * (1.0 + 3.0 * b * square)
        d_pre = (d_hidden * slope).astype(BF16)
        d_ref[t] = d_pre
        sums = jnp.sum(d_pre.astype(F32), axis=0, keepdims=True)
        sum_ref[t] = jnp.broadcast_to(sums, sum_ref.shape[1:])
        blocks.append(d_pre)
    turned_product(blocks, fc_ref, into_parts(parts))


def feed_back(sources, fc, proj, pre):
    return call(
        feed_back_kernel,
        "feed_back",
        (1,),
        [whole(s) for s in sources] + [weight_of(fc), weight_of(proj), whole(pre)],
        [
            out_whole((SEEN, WIDTH), BF16),
            out_whole((4, SEEN, 256), BF16),
            out_whole((4, 8, 256), F32),
            *out_parts(),
        ],
        flops=8 * SEEN * WIDTH * 1024,
        exps=SEEN * 1024,
    )


def small_rows(d, t, refs):
    fc0, fc1, qkvo0, qkvo1, attn0, feed0, attn1, feed1, last = refs
    lanes = slice(d * 128, (d + 1) * 128)

    def pair(one, first, two, second):
        return jnp.concatenate(
            [one[first : first + 1, lanes], two[second : second + 1, lanes]], axis=1
        )

    rows = [fc0[t, 0:1], fc1[t, 0:1], qkvo0[t, 0:1], qkvo1[t, 0:1]]
    for attn, feed, after in ((attn0, feed0, attn1), (attn1, feed1, last)):
        rows += [
            pair(attn, 0, feed, 0),
            pair(attn, 1, feed, 1),
            pair(feed, 2, after, 2),
        ]
    return rows


def weight_grad_kernel(attention, extra, me_ref, a_ref, ab_ref, b_ref, bb_ref, *refs):
    own_ref, other_ref = refs[-2:]
    left, right = a_ref[...].T, b_ref[...].T
    for out, core in ((own_ref, 0), (other_ref, 1)):
        for x in range(2):
            t = (x ^ me_ref[1]) * 2 + (core ^ me_ref[2])
            one = jnp.dot(left, ab_ref[t], preferred_element_type=F32)
            two = jnp.dot(right, bb_ref[t], preferred_element_type=F32)
            for d in range(8):
                to = d ^ me_ref[0]
                rows = slice(d * 128, (d + 1) * 128)
                if attention:
                    out[x, to, :128, :128] = one[rows, :128].astype(BF16)
                    out[x, to, :128, 128:] = (one[rows, 128:] + two[rows]).astype(BF16)
                else:
                    out[x, to, :128] = one[rows].astype(BF16)
                    out[x, to, 128:] = two[rows].astype(BF16)
                if extra:
                    small = small_rows(d, t, refs[:-2])
                    small.append(jnp.zeros((16 - len(small), 256), F32))
                    out[x, to, 128:] = jnp.concatenate(small, axis=0).astype(BF16)


def weight_grads(attention, me, a, a_blocks, b, b_blocks, extra=()):
    rows = (128 if attention else 256) + (16 if extra else 0)
    arrays = [a, a_blocks, b, b_blocks, *extra]
    own, other = call(
        functools.partial(weight_grad_kernel, attention, len(extra) > 0),
        "weight_grads",
        (1,),
        [whole(array) for array in arrays],
        [out_whole((2, 8, rows, 256), BF16)] * 2,
        flops=7 * SEEN * WIDTH * 1024,
        prefetch=me,
    )
    return own.reshape(4, 4, rows, 256), other.reshape(4, 4, rows, 256)


def after_core_kernel(own_ref, got_ref, keep_ref, *sends):
    keep_ref[0] = own_ref[0, 0].astype(F32) + got_ref[0, 0].astype(F32)
    for k, send in enumerate(sends):
        send[0] = (own_ref[k + 1, 0].astype(F32) + got_ref[k + 1, 0].astype(F32)).astype(BF16)


def after_core(own, got):
    rows = own.shape[2]

    def at(y):
        return (0, y, 0, 0)

    def to(y):
        return (y, 0, 0)

    shape, block = (4, rows, 256), (1, rows, 256)
    keep, *sends = call(
        after_core_kernel,
        "after_core",
        (4,),
        [(own, (4, 1, rows, 256), at), (got, (4, 1, rows, 256), at)],
        [(shape, F32, block, to)] + [(shape, BF16, block, to)] * 3,
        flops=own.size,
    )
    return keep, sends


def after_x_kernel(keep_ref, one, two, three, out_ref, *sends):
    for y in range(4):
        value = keep_ref[y] + one[y].astype(F32) + two[y].astype(F32) + three[y].astype(F32)
        if y == 0:
            out_ref[...] = value
        else:
            sends[y - 1][...] = value.astype(BF16)


def after_x(keep, got):
    shape = keep.shape[1:]
    keep, *sends = call(
        after_x_kernel,
        "after_x",
        (1,),
        [whole(keep)] + [whole(g) for g in got],
        [out_whole(shape, F32)] + [out_whole(shape, BF16)] * 3,
        flops=keep.size * 3,
    )
    return keep, sends


def finish_feed_kernel(*refs):
    fc_ref, proj_ref = refs[-2:]
    for i in range(2):
        value = total_of(refs[4 * i : 4 * i + 4])
        fc_ref[i] = value[:128]
        proj_ref[i] = value[128:].T


def finish_feed(groups):
    return call(
        finish_feed_kernel,
        "finish_feed",
        (1,),
        [whole(a) for group in groups for a in group],
        [out_whole((2, 128, 256), F32), out_whole((2, 256, 128), F32)],
        flops=1 << 19,
    )


def finish_attention_kernel(*refs):
    qkv_ref, out_ref, small_ref = refs[-3:]
    for i in range(2):
        value = total_of(refs[4 * i : 4 * i + 4])
        qkv_ref[i, 0] = value[:128, 128:192]
        qkv_ref[i, 1] = value[:128, :64]
        qkv_ref[i, 2] = value[:128, 64:128]
        out_ref[i] = value[:128, 128:].T[64:]
        if i == 0:
            small_ref[...] = value[128:]


def finish_attention(groups):
    return call(
        finish_attention_kernel,
        "finish_attention",
        (1,),
        [whole(a) for group in groups for a in group],
        [
            out_whole((2, 3, 128, 64), F32),
            out_whole((2, 64, 128), F32),
            out_whole((16, 256), F32),
        ],
        flops=1 << 19,
    )


def pack_kernel(qkv_ref, wo_ref, fc_ref, proj_ref, bq_ref, bf_ref, gain_ref, shift_ref, *outs):
    early_ref, late_ref, last_ref = outs

    def attention(i):
        pieces = [qkv_ref[i, 1], qkv_ref[i, 2], qkv_ref[i, 0], wo_ref[i].T]
        return jnp.concatenate(pieces, axis=1)

    early_ref[:128] = attention(0)
    rows = []
    for i in range(2):
        none = jnp.zeros((1, 80), BF16)
        rows.append(jnp.concatenate([bq_ref[i, 0], bq_ref[i, 1], bf_ref[i], none], axis=1))
        rows += [gain_ref[i], shift_ref[i], jnp.zeros((1, 128), BF16)]
    small = jnp.concatenate([r.astype(F32) for r in rows], axis=0)
    small = jnp.concatenate([small, jnp.zeros_like(small)], axis=1)
    early_ref[128:] = small.astype(BF16)
    late_ref[:128] = fc_ref[0]
    late_ref[128:256] = proj_ref[0].T
    late_ref[256:] = attention(1)
    last_ref[:128] = fc_ref[1]
    last_ref[128:] = proj_ref[1].T


def pack(*arrays):
    return call(
        pack_kernel,
        "pack",
        (1,),
        [whole(a) for a in arrays],
        [
            out_whole((144, 256), BF16),
            out_whole((384, 256), BF16),
            out_whole((256, 256), BF16),
        ],
    )


def merge_kernel(me_ref, own_ref, other_ref, out_ref):
    for d in range(8):
        for ref, core in ((own_ref, 0), (other_ref, 1)):
            for x in range(2):
                t = (x ^ me_ref[1]) * 2 + (core ^ me_ref[2])
                out_ref[d, t] = ref[x, d ^ me_ref[0]]


def merge(me, own, other):
    return call(
        merge_kernel,
        "merge",
        (1,),
        [whole(own), whole(other)],
        [out_whole((8, 4, *own.shape[2:]), BF16)],
        prefetch=me,
    )[0]


def total_of(parts):
    value = parts[0][...].astype(F32)
    for part in parts[1:]:
        value = value + part[...].astype(F32)
    return value


def residual_kernel(p0, p1, p2, p3, x_ref, bias_ref, gain_ref, shift_ref, next_ref, norm_ref):
    value = x_ref[...].astype(F32) + total_of((p0, p1, p2, p3)) + bias_ref[0:1]
    next_ref[...] = value
    norm_ref[...] = (xhat_of(value)[0] * gain_ref[0:1] + shift_ref[0:1]).astype(BF16)


def add_and_norm(parts, values, bias, gain, shift):
    return call(
        residual_kernel,
        "add_and_norm",
        (1,),
        [whole(p) for p in parts] + [whole(values), whole(bias), whole(gain), whole(shift)],
        [out_whole((OWN, WIDTH), F32), out_whole((OWN, WIDTH), BF16)],
        flops=OWN * WIDTH * 16,
    )


def norm_back_kernel(p0, p1, p2, p3, x_ref, gain_ref, g_ref, out_ref, low_ref, sum_ref):
    grad = total_of((p0, p1, p2, p3))
    xhat, rstd = xhat_of(x_ref[...].astype(F32))
    dxhat = grad * gain_ref[0:1]
    into = dxhat - jnp.mean(dxhat, axis=-1, keepdims=True)
    into = (into - xhat * jnp.mean(dxhat * xhat, axis=-1, keepdims=True)) * rstd
    value = g_ref[...].astype(F32) + into
    out_ref[...] = value
    low = value.astype(BF16)
    low_ref[...] = low
    sum_ref[...] = jnp.zeros_like(sum_ref)
    sum_ref[0:1] = jnp.sum(grad * xhat, axis=0, keepdims=True)
    sum_ref[1:2] = jnp.sum(grad, axis=0, keepdims=True)
    sum_ref[2:3] = jnp.sum(low.astype(F32), axis=0, keepdims=True)


def norm_back(parts, values, gain, grad):
    return call(
        norm_back_kernel,
        "norm_back",
        (1,),
        [whole(p) for p in parts] + [whole(values), whole(gain), whole(grad)],
        [
            out_whole((OWN, WIDTH), F32),
            out_whole((OWN, WIDTH), BF16),
            out_whole((8, WIDTH), F32),
        ],
        flops=OWN * WIDTH * 32,
    )


def on_device(
    tokens, segments, cotangent, w_qkv, b_qv, w_out, w_fc, b_fc, w_proj, norm_gains, shifts
):
    layers = w_qkv.shape[0]
    xl, y, xh, z, core = (lax.axis_index(a) for a in ("xl", "y", "xh", "z", "c"))
    d_own = xl * 4 + y
    me = jnp.stack([d_own, xh, core]).astype(jnp.int32)
    first = xh == 0
    block = tokens.shape[0]

    def by_row(value):
        kept = jnp.where(first, value[:, 0], value[:, 1])
        got = swap(jnp.where(first, value[:, 1], value[:, 0]), "xh", 1)
        return jnp.concatenate(
            [jnp.where(first, kept, got), jnp.where(first, got, kept)], axis=0
        )

    def by_position(value):
        lower, upper = value[:block], value[block:]
        kept = jnp.where(first, lower, upper)
        got = swap(jnp.where(first, upper, lower).astype(BF16), "xh", 1).astype(value.dtype)
        return jnp.stack([jnp.where(first, kept, got), jnp.where(first, got, kept)], axis=1)

    own_tokens = by_row(tokens)

    early, late, last = pack(w_qkv, w_out, w_fc, w_proj, b_qv, b_fc, norm_gains, shifts)
    one, three, two = (swap(early, "y", k) for k in (1, 3, 2))
    early = jnp.stack([early, one, two, three])
    early, own_tokens, late = tied(early, own_tokens, late)
    all_tokens = over_z(own_tokens)
    low, high, both = swaps_x([early] * 3)
    low, high, both, all_tokens = tied(low, high, both, all_tokens)
    early = jnp.stack([early, low, high, both]).reshape(2, 8, *early.shape[1:])
    early = merge(me, early, swap(early, "c", 1))
    late = lax.all_gather(late, PLANE, axis=0, tiled=False).reshape(8, 4, *late.shape)
    last = lax.all_gather(last, PLANE, axis=0, tiled=False).reshape(8, 4, *last.shape)
    attn_w = [(early, 0), (late, 2)]
    fc_w = [(late, 0), (last, 0)]
    proj_w = [(late, 1), (last, 1)]

    small_all = early[:, :, 128:, :128].reshape(8, 4, layers, 8, 128).transpose(2, 1, 3, 0, 4)
    rows = small_all[:, 0, 1:7].reshape(layers, 6, 1, WIDTH).astype(F32)
    rows = jnp.broadcast_to(rows, (layers, 6, 8, WIDTH))
    gains = [[rows[i, k] for k in range(2)] for i in range(layers)]
    shift = [[rows[i, 2 + k] for k in range(4)] for i in range(layers)]
    biases = small_all[:, :, 0].astype(F32)
    q_bias = biases[..., :8].reshape(layers, 4, HD)
    v_bias = biases[..., 8:16].reshape(layers, 4, HD)
    fc_bias = biases[..., 16:48].reshape(layers, 4, 1, 256)
    fc_bias = jnp.broadcast_to(fc_bias, (layers, 4, 8, 256))
    none = jnp.zeros_like(q_bias)
    qkvo_bias = jnp.concatenate([none, v_bias, q_bias, none], axis=2)[:, :, None]
    qkvo_bias = jnp.broadcast_to(qkvo_bias, (layers, 4, 8, 256))
    column = jnp.arange(256)
    scale = jnp.where(column < 2 * HD, 1.0, jnp.where(column < 3 * HD, 0.125, 0.0))
    scale = jnp.broadcast_to(scale.astype(F32), (8, 256))

    seg_row = jnp.where(first, segments[0], segments[1])
    position = jnp.arange(seg_row.shape[0], dtype=jnp.int32)

    def at_core(value, which):
        cut = value.reshape(2, 4, 2, block)
        cut = jnp.where(which == 0, cut[:, :, 0], cut[:, :, 1])
        for bit in (1, 2):
            turned = jnp.stack([cut[:, k ^ bit] for k in range(4)], axis=1)
            cut = jnp.where((z & bit) != 0, turned, cut)
        return cut.reshape(2, 4 * block)

    own_pos, own_seg = at_core(position, core), at_core(seg_row, core)
    par_pos, par_seg = at_core(position, 1 - core), at_core(seg_row, 1 - core)
    q_pos, q_seg = own_pos.reshape(-1, 1), own_seg.reshape(-1, 1)
    k_pos = jnp.concatenate([own_pos, par_pos], axis=1).reshape(1, -1)
    k_seg = jnp.concatenate([own_seg, par_seg], axis=1).reshape(1, -1)
    bias = jnp.where((q_seg == k_seg) & (q_pos >= k_pos), 0.0, -1e30).astype(F32)

    kept = []
    residual, normed = own_tokens, None
    low = by_row(cotangent)
    for i in range(layers):
        attn_input = residual
        if i == 0:
            sources, norm = all_tokens, (gains[i][0], shift[i][0])
        else:
            sources, norm = over_z(normed), ()
        attn_rows, queries, kv = project(sources, norm, attn_w[i], qkvo_bias[i], scale)
        par = swap(kv, "c", 1)
        if i == 0:
            _, *cotangents = over_z(low)
        mixed, lse, *parts = attend(queries, kv, par, bias, attn_w[i])
        if i == 0:
            parts, cotangents[1] = tied(parts, cotangents[1])
        else:
            parts, cotangents = tied(parts, cotangents)
        residual, normed = add_and_norm(
            exchanged(parts), residual, shift[i][2], gains[i][1], shift[i][1]
        )
        mlp_input = residual
        mlp_rows, pre, hidden, *parts = feed(over_z(normed), fc_w[i], proj_w[i], fc_bias[i])
        after = min(i + 1, layers - 1)
        if i == layers - 1:
            last_parts = exchanged(parts)
        else:
            residual, normed = add_and_norm(
                exchanged(parts), residual, shift[i][3], gains[after][0], shift[after][0]
            )
        kept.append(
            (attn_input, attn_rows, queries, kv, par, mixed, lse, mlp_input, mlp_rows, pre, hidden)
        )
    gradient = low
    sums = jnp.sum(low.astype(F32), axis=0, keepdims=True)
    last_sums = jnp.concatenate([jnp.zeros((2, WIDTH), F32), sums, jnp.zeros((5, WIDTH), F32)])
    feed_shards, attn_shards = [None] * layers, [None] * layers
    small_sums = [None] * layers
    attn_x = None
    for i in reversed(range(layers)):
        (attn_input, attn_rows, queries, kv, par, mixed, lse, mlp_input, mlp_rows, pre, hidden) = (
            kept[i]
        )
        if i == layers - 1:
            sources = (low, *cotangents)
        else:
            got = swaps_x(attn_x[1])
            sources, got = tied(over_z(low), got)
            done = after_x(attn_x[0], got)
            attn_shards[i + 1] = (done[0], *swaps_y(done[1]))
        grad_rows, d_pre, fc_sum, *parts = feed_back(sources, fc_w[i], proj_w[i], pre)
        feed_grads = weight_grads(False, me, mlp_rows, d_pre, grad_rows, hidden)
        feed_x = after_core(feed_grads[0], swap(feed_grads[1], "c", 1))
        parts, feed_x = tied(exchanged(parts), feed_x)
        if i < layers - 1:
            parts, attn_shards[i + 1] = tied(parts, attn_shards[i + 1])
        gradient, low, feed_sums = norm_back(parts, mlp_input, gains[i][1], gradient)
        got = swaps_x(feed_x[1])
        grad_rows, dq, own_dkv, other_dkv = attend_back(
            over_z(low), attn_w[i], queries, kv, par, bias, lse
        )
        other_dkv, got, last_parts = tied(other_dkv, got, last_parts)
        if i == layers - 1:
            last, _ = add_and_norm(last_parts, residual, shift[i][3], gains[i][0], shift[i][0])
            output = by_position(last.astype(BF16))
        got_dkv = swap(other_dkv, "c", 1)
        done = after_x(feed_x[0], got)
        feed_shards[i] = (done[0], *swaps_y(done[1]))
        d_qkvo, qkvo_sum, *parts = rejoin(
            own_dkv, got_dkv, dq, attn_w[i], all_tokens if i == 0 else ()
        )
        small_sums[i] = [fc_sum, qkvo_sum, feed_sums]
        if i > 0:
            attn_grads = weight_grads(True, me, attn_rows, d_qkvo, grad_rows, mixed)
            attn_x = after_core(attn_grads[0], swap(attn_grads[1], "c", 1))
            parts, attn_x, feed_shards[i] = tied(exchanged(parts), attn_x, feed_shards[i])
            gradient, low, sums = norm_back(parts, attn_input, gains[i][0], gradient)
            small_sums[i].append(sums)
        else:
            small_sums[i].append(parts.pop())
    (fc0, qkvo0, feed0, attn0), (fc1, qkvo1, feed1, attn1) = small_sums
    extra = (fc0, fc1, qkvo0, qkvo1, attn0, feed0, attn1, feed1, last_sums)
    attn_grads = weight_grads(True, me, attn_rows, d_qkvo, grad_rows, mixed, extra)
    attn_x = after_core(attn_grads[0], swap(attn_grads[1], "c", 1))
    parts, attn_x = tied(exchanged(parts), attn_x)
    got = swaps_x(attn_x[1])
    gradient, _, _ = norm_back(parts, attn_input, gains[0][0], gradient)
    done = after_x(attn_x[0], got)
    attn_shards[0] = (done[0], *swaps_y(done[1]))
    g_tokens = by_position(gradient)
    g_w_fc, g_w_proj = finish_feed(feed_shards)
    g_w_qkv, g_w_out, mine = finish_attention(attn_shards)
    everywhere = sum(over_z(mine))
    g_b_fc = lax.dynamic_slice_in_dim(mine[:2], d_own * 32, 32, 1).reshape(layers, 1, 32)
    bias_sums = jnp.stack([mine[2:4, 128:192], mine[2:4, 64:128]], axis=1)
    g_b_qv = lax.dynamic_slice_in_dim(bias_sums, d_own * 8, 8, 2).reshape(layers, 2, 1, 8)
    vectors = everywhere[4:10].reshape(layers, 3, 2, 128)
    g_norm_gains = vectors[:, 0]
    g_shifts = jnp.concatenate([vectors[:, 1], vectors[:, 2]], axis=1)
    return (
        output,
        g_tokens,
        g_w_qkv,
        g_b_qv,
        g_w_out,
        g_w_fc,
        g_b_fc,
        g_w_proj,
        g_norm_gains,
        g_shifts,
    )


def solution(mesh):
    split = Mesh(mesh.devices.reshape(2, 4, 2, 4, 2), ("xl", "y", "xh", "z", "c"))
    dp, tensor = ("xl", "y"), ("xh", "z", "c")
    rows = P(tensor, dp, None)
    weights = (
        P(None, None, dp, tensor),
        P(None, None, tensor, dp),
        P(None, tensor, dp),
        P(None, dp, tensor),
        P(None, tensor, dp),
        P(None, tensor, dp),
        P(None, None, dp),
        P(None, None, dp),
    )
    return jax.shard_map(
        on_device,
        mesh=split,
        in_specs=(rows, P(dp, None), rows, *weights),
        out_specs=(rows, rows, *weights),
        check_vma=False,
    )
```

```python
import functools

import jax
import jax.numpy as jnp
from jax import lax
from jax.experimental import pallas as pl
from jax.experimental.pallas import tpu as pltpu
from jax.sharding import Mesh
from jax.sharding import PartitionSpec as P

EPS = 1e-05
F32 = jnp.float32
BF16 = jnp.bfloat16
X = ("xl", "xh")
PLANE = ("xl", "y", "xh", "c")
HD = 64
OWN = 128
SEEN = 512
WIDTH = 1024
VMEM = 20 << 20
NT = (((1,), (1,)), ((), ()))
TN = (((0,), (0,)), ((), ()))


def swap(value, axis, mask):
    count = lax.axis_size(axis)
    return lax.ppermute(value, axis, [(i, i ^ mask) for i in range(count)])


def over_z(value):
    two, one, three = (swap(value, "z", k) for k in (2, 1, 3))
    return value, one, two, three


def exchanged(parts):
    two, one, three = (swap(parts[k], "z", k) for k in (2, 1, 3))
    return parts[0], one, two, three


def tied(*values):
    return lax.optimization_barrier(values)


def swaps_x(parts):
    return [swap(part, X, mask) for part, mask in zip(parts, (2, 1, 3))]


def swaps_y(parts):
    one, three, two = (swap(parts[k - 1], "y", k) for k in (1, 3, 2))
    return one, two, three


def call(kernel, name, grid, ins, outs, scratch=(), flops=0, exps=0, prefetch=None, vmem=VMEM):
    arrays = [a for a, _, _ in ins]
    in_specs = [pl.BlockSpec(block, index) for _, block, index in ins]
    out_specs = [pl.BlockSpec(block, index) for _, _, block, index in outs]
    shapes = [jax.ShapeDtypeStruct(shape, kind) for shape, kind, _, _ in outs]
    moved = sum(a.size * a.dtype.itemsize for a in arrays)
    moved += sum(s.size * s.dtype.itemsize for s in shapes)
    keys = dict(
        out_shape=shapes,
        name=name,
        compiler_params=pltpu.CompilerParams(vmem_limit_bytes=vmem),
        cost_estimate=pl.CostEstimate(
            flops=flops // 10, bytes_accessed=moved // 10, transcendentals=exps // 10
        ),
    )
    if prefetch is None:
        return pl.pallas_call(
            kernel,
            grid=grid,
            in_specs=in_specs,
            out_specs=out_specs,
            scratch_shapes=list(scratch),
            **keys,
        )(*arrays)
    spec = pltpu.PrefetchScalarGridSpec(
        num_scalar_prefetch=1,
        grid=grid,
        in_specs=in_specs,
        out_specs=out_specs,
        scratch_shapes=list(scratch),
    )
    return pl.pallas_call(kernel, grid_spec=spec, **keys)(prefetch, *arrays)


def whole(array):
    return (array, array.shape, lambda *_: (0,) * array.ndim)


def weight_of(store, lanes=256, column=0):
    array, row = store
    return (array, (8, 4, 128, lanes), lambda *_: (0, 0, row, column))


def out_whole(shape, kind):
    return (shape, kind, shape, lambda *_: (0,) * len(shape))


def out_parts():
    return [out_whole((OWN, WIDTH), BF16)] * 4


def matrix(ref, t):
    return ref[:, t].reshape(8 * ref.shape[2], ref.shape[3])


def turned_product(blocks, ref, emit):
    left = jnp.concatenate(blocks, axis=1)
    for d in range(4):
        pieces = [
            ref[2 * d : 2 * d + 2, t].reshape(2 * ref.shape[2], ref.shape[3]) for t in range(4)
        ]
        right = jnp.concatenate(pieces, axis=1)
        value = lax.dot_general(left, right, NT, preferred_element_type=F32)
        emit(slice(d * 256, (d + 1) * 256), value)


def into_parts(parts):
    def emit(columns, value):
        for k, part in enumerate(parts):
            part[:, columns] = value[k * OWN : (k + 1) * OWN].astype(BF16)

    return emit


def xhat_of(values):
    center = values - jnp.mean(values, axis=-1, keepdims=True)
    rstd = lax.rsqrt(jnp.mean(center * center, axis=-1, keepdims=True) + EPS)
    return center * rstd, rstd


def fill_rows(sources, rows_ref, gain_ref=None, shift_ref=None):
    for k, source in enumerate(sources):
        value = source[...]
        if gain_ref is not None:
            value = xhat_of(value.astype(F32))[0] * gain_ref[0:1] + shift_ref[0:1]
            value = value.astype(BF16)
        rows_ref[k * OWN : (k + 1) * OWN] = value


def project_kernel(normalize, *refs):
    sources, refs = refs[:4], refs[4:]
    gain_ref, shift_ref = None, None
    if normalize:
        (gain_ref, shift_ref), refs = refs[:2], refs[2:]
    w_ref, bias_ref, scale_ref, rows_ref, q_ref, kv_ref = refs
    fill_rows(sources, rows_ref, gain_ref, shift_ref)
    for t in range(4):
        value = jnp.dot(rows_ref[...], matrix(w_ref, t), preferred_element_type=F32)
        value = ((value + bias_ref[t, 0:1]) * scale_ref[0:1]).astype(BF16)
        q_ref[t] = value[:, 128:]
        kv_ref[t] = value[:, :128]


def project(sources, norm, store, bias, scale):
    ins = [whole(s) for s in sources] + [whole(n) for n in norm]
    ins += [weight_of(store), whole(bias), whole(scale)]
    return call(
        functools.partial(project_kernel, len(norm) > 0),
        "project",
        (1,),
        ins,
        [out_whole((SEEN, WIDTH), BF16)] + [out_whole((4, SEEN, 128), BF16)] * 2,
        flops=2 * SEEN * WIDTH * 1024,
    )


def half_rows(value, part):
    step = OWN // 2
    return jnp.concatenate(
        [value[k * OWN + part * step : k * OWN + (part + 1) * step] for k in range(4)], axis=0
    )


def store_half(ref, t, part, value):
    step = OWN // 2
    for k in range(4):
        ref[t, k * OWN + part * step : k * OWN + (part + 1) * step] = value[
            k * step : (k + 1) * step
        ]


def head_keys(kv, par):
    return jnp.concatenate(
        [half_rows(kv, 0), half_rows(par, 0), half_rows(kv, 1), half_rows(par, 1)], axis=0
    )


def attend_kernel(kv_ref, par_ref, q_ref, bias_ref, w_ref, mixed_ref, lse_ref, *parts):
    half = SEEN // 2
    for t in range(4):
        kv = head_keys(kv_ref[t], par_ref[t])
        queries = q_ref[t]
        for part in range(2):
            rows = slice(part * half, (part + 1) * half)
            seen = SEEN * (part + 1)
            keys = kv[:seen]
            scores = lax.dot_general(
                half_rows(queries, part), keys, NT, preferred_element_type=F32
            )
            scores = scores + bias_ref[rows, :seen]
            highest = jnp.max(scores, axis=1, keepdims=True)
            raised = jnp.exp(scores - highest)
            totals = jnp.sum(raised, axis=1, keepdims=True)
            probs = (raised * (1.0 / totals)).astype(BF16)
            mixed = jnp.dot(probs, keys, preferred_element_type=F32)
            lane = lax.broadcasted_iota(jnp.int32, mixed.shape, 1)
            store_half(mixed_ref, t, part, jnp.where(lane >= HD, mixed, 0.0).astype(BF16))
            lse_ref[t, rows] = highest + jnp.log(totals)
    turned_product([mixed_ref[t] for t in range(4)], w_ref, into_parts(parts))


AREA = 4 * SEEN * 768


def attend(queries, kv, par, bias, store):
    return call(
        attend_kernel,
        "attend",
        (1,),
        [whole(kv), whole(par), whole(queries), whole(bias), weight_of(store, 128, 1)],
        [
            out_whole((4, SEEN, 128), BF16),
            out_whole((4, SEEN, 1), F32),
            *out_parts(),
        ],
        flops=AREA * 3700,
        exps=AREA,
    )


def attend_back_kernel(g0, g1, g2, g3, w_ref, kv_ref, par_ref, q_ref, bias_ref, lse_ref, *outs):
    rows_ref, dq_ref, own_ref, other_ref = outs
    fill_rows((g0, g1, g2, g3), rows_ref)
    half = SEEN // 2
    for t in range(4):
        d_mixed = jnp.dot(rows_ref[...], matrix(w_ref, t), preferred_element_type=F32)
        lane = lax.broadcasted_iota(jnp.int32, d_mixed.shape, 1)
        d_mixed = jnp.where(lane >= HD, d_mixed, 0.0).astype(BF16)
        kv = head_keys(kv_ref[t], par_ref[t])
        all_queries = q_ref[t]
        sums = []
        for part in range(2):
            rows = slice(part * half, (part + 1) * half)
            seen = SEEN * (part + 1)
            keys = kv[:seen]
            queries = half_rows(all_queries, part)
            grad = half_rows(d_mixed, part)
            scores = lax.dot_general(queries, keys, NT, preferred_element_type=F32)
            probs = jnp.exp(scores + bias_ref[rows, :seen] - lse_ref[t, rows])
            dprobs = lax.dot_general(grad, keys, NT, preferred_element_type=F32)
            inner = jnp.sum(probs * dprobs, axis=1, keepdims=True)
            dscores = (probs * (dprobs - inner)).astype(BF16)
            low = probs.astype(BF16)
            dq = jnp.dot(dscores, keys, preferred_element_type=F32) * 0.125
            lane = lax.broadcasted_iota(jnp.int32, dq.shape, 1)
            store_half(dq_ref, t, part, jnp.where(lane < HD, dq, 0.0).astype(BF16))
            sums.append(
                lax.dot_general(dscores, queries, TN, preferred_element_type=F32)
                + lax.dot_general(low, grad, TN, preferred_element_type=F32)
            )
        lower = sums[0] + sums[1][:SEEN]
        upper = sums[1][SEEN:]
        for part, value in enumerate((lower, upper)):
            store_half(own_ref, t, part, value[:half])
            store_half(other_ref, t, part, value[half:].astype(BF16))


def attend_back(sources, store, queries, kv, par, bias, lse):
    return call(
        attend_back_kernel,
        "attend_back",
        (1,),
        [whole(s) for s in sources]
        + [weight_of(store, 128, 1)]
        + [whole(a) for a in (kv, par, queries, bias, lse)],
        [
            out_whole((SEEN, WIDTH), BF16),
            out_whole((4, SEEN, 128), BF16),
            out_whole((4, SEEN, 128), F32),
            out_whole((4, SEEN, 128), BF16),
        ],
        flops=AREA * 6200,
        exps=AREA,
    )


def rejoin_kernel(norm_sums, own_ref, got_ref, dq_ref, w_ref, *refs):
    tokens, refs = refs[: 4 * norm_sums], refs[4 * norm_sums :]
    d_ref, sum_ref, p0, p1, p2, p3, *rest = refs
    for t in range(4):
        dkv = (own_ref[t] + got_ref[t].astype(F32)).astype(BF16)
        value = jnp.concatenate([dkv, dq_ref[t]], axis=1)
        d_ref[t] = value
        sums = jnp.sum(value.astype(F32), axis=0, keepdims=True)
        sum_ref[t] = jnp.broadcast_to(sums, sum_ref.shape[1:])
    blocks = [d_ref[t] for t in range(4)]
    emit = into_parts((p0, p1, p2, p3))
    if not norm_sums:
        turned_product(blocks, w_ref, emit)
        return
    norm_ref, xhat_ref = rest
    for k in range(4):
        xhat_ref[k * OWN : (k + 1) * OWN] = xhat_of(tokens[k][...].astype(F32))[0]
    norm_ref[...] = jnp.zeros_like(norm_ref)

    def emit_sums(columns, value):
        emit(columns, value)
        norm_ref[0:1, columns] = jnp.sum(value * xhat_ref[:, columns], axis=0, keepdims=True)
        norm_ref[1:2, columns] = jnp.sum(value, axis=0, keepdims=True)

    turned_product(blocks, w_ref, emit_sums)


def rejoin(own, got, dq, store, tokens=()):
    outs = [out_whole((4, SEEN, 256), BF16), out_whole((4, 8, 256), F32), *out_parts()]
    scratch = []
    if tokens:
        outs.append(out_whole((8, WIDTH), F32))
        scratch.append(pltpu.VMEM((SEEN, WIDTH), F32))
    return call(
        functools.partial(rejoin_kernel, len(tokens) > 0),
        "rejoin",
        (1,),
        [whole(own), whole(got), whole(dq), weight_of(store)] + [whole(t) for t in tokens],
        outs,
        scratch,
        flops=2 * SEEN * WIDTH * 1024,
    )


def gelu_parts(pre):
    a, b = 0.7978845608028654, 0.044715
    square = pre * pre
    return square, jnp.tanh(a * pre * (1.0 + b * square)), a, b


def feed_kernel(x0, x1, x2, x3, fc_ref, proj_ref, bias_ref, rows_ref, pre_ref, hid_ref, *parts):
    fill_rows((x0, x1, x2, x3), rows_ref)
    blocks = []
    for t in range(4):
        pre = jnp.dot(rows_ref[...], matrix(fc_ref, t), preferred_element_type=F32)
        pre = pre + bias_ref[t, 0:1]
        pre_ref[t] = pre
        _, th, _, _ = gelu_parts(pre)
        hidden = (0.5 * pre * (1.0 + th)).astype(BF16)
        hid_ref[t] = hidden
        blocks.append(hidden)
    turned_product(blocks, proj_ref, into_parts(parts))


def feed(sources, fc, proj, bias):
    return call(
        feed_kernel,
        "feed",
        (1,),
        [whole(s) for s in sources] + [weight_of(fc), weight_of(proj), whole(bias)],
        [
            out_whole((SEEN, WIDTH), BF16),
            out_whole((4, SEEN, 256), F32),
            out_whole((4, SEEN, 256), BF16),
            *out_parts(),
        ],
        flops=8 * SEEN * WIDTH * 1024,
        exps=SEEN * 1024,
    )


def feed_back_kernel(g0, g1, g2, g3, fc_ref, proj_ref, pre_ref, rows_ref, d_ref, sum_ref, *parts):
    fill_rows((g0, g1, g2, g3), rows_ref)
    blocks = []
    for t in range(4):
        d_hidden = jnp.dot(rows_ref[...], matrix(proj_ref, t), preferred_element_type=F32)
        pre = pre_ref[t]
        square, th, a, b = gelu_parts(pre)
        slope = 0.5 * (1.0 + th) + 0.5 * pre * (1.0 - th * th) * a * (1.0 + 3.0 * b * square)
        d_pre = (d_hidden * slope).astype(BF16)
        d_ref[t] = d_pre
        sums = jnp.sum(d_pre.astype(F32), axis=0, keepdims=True)
        sum_ref[t] = jnp.broadcast_to(sums, sum_ref.shape[1:])
        blocks.append(d_pre)
    turned_product(blocks, fc_ref, into_parts(parts))


def feed_back(sources, fc, proj, pre):
    return call(
        feed_back_kernel,
        "feed_back",
        (1,),
        [whole(s) for s in sources] + [weight_of(fc), weight_of(proj), whole(pre)],
        [
            out_whole((SEEN, WIDTH), BF16),
            out_whole((4, SEEN, 256), BF16),
            out_whole((4, 8, 256), F32),
            *out_parts(),
        ],
        flops=8 * SEEN * WIDTH * 1024,
        exps=SEEN * 1024,
    )


def small_rows(d, t, refs):
    fc0, fc1, qkvo0, qkvo1, attn0, feed0, attn1, feed1, last = refs
    lanes = slice(d * 128, (d + 1) * 128)

    def pair(one, first, two, second):
        return jnp.concatenate(
            [one[first : first + 1, lanes], two[second : second + 1, lanes]], axis=1
        )

    rows = [fc0[t, 0:1], fc1[t, 0:1], qkvo0[t, 0:1], qkvo1[t, 0:1]]
    for attn, feed, after in ((attn0, feed0, attn1), (attn1, feed1, last)):
        rows += [
            pair(attn, 0, feed, 0),
            pair(attn, 1, feed, 1),
            pair(feed, 2, after, 2),
        ]
    return rows


def weight_grad_kernel(attention, extra, me_ref, a_ref, ab_ref, b_ref, bb_ref, *refs):
    own_ref, other_ref = refs[-2:]
    left, right = a_ref[...].T, b_ref[...].T
    for out, core in ((own_ref, 0), (other_ref, 1)):
        for x in range(2):
            t = (x ^ me_ref[1]) * 2 + (core ^ me_ref[2])
            one = jnp.dot(left, ab_ref[t], preferred_element_type=F32)
            two = jnp.dot(right, bb_ref[t], preferred_element_type=F32)
            for d in range(8):
                to = d ^ me_ref[0]
                rows = slice(d * 128, (d + 1) * 128)
                if attention:
                    out[x, to, :128, :128] = one[rows, :128].astype(BF16)
                    out[x, to, :128, 128:] = (one[rows, 128:] + two[rows]).astype(BF16)
                else:
                    out[x, to, :128] = one[rows].astype(BF16)
                    out[x, to, 128:] = two[rows].astype(BF16)
                if extra:
                    small = small_rows(d, t, refs[:-2])
                    small.append(jnp.zeros((16 - len(small), 256), F32))
                    out[x, to, 128:] = jnp.concatenate(small, axis=0).astype(BF16)


def weight_grads(attention, me, a, a_blocks, b, b_blocks, extra=()):
    rows = (128 if attention else 256) + (16 if extra else 0)
    arrays = [a, a_blocks, b, b_blocks, *extra]
    own, other = call(
        functools.partial(weight_grad_kernel, attention, len(extra) > 0),
        "weight_grads",
        (1,),
        [whole(array) for array in arrays],
        [out_whole((2, 8, rows, 256), BF16)] * 2,
        flops=7 * SEEN * WIDTH * 1024,
        prefetch=me,
    )
    return own.reshape(4, 4, rows, 256), other.reshape(4, 4, rows, 256)


def after_core_kernel(own_ref, got_ref, keep_ref, *sends):
    keep_ref[0] = own_ref[0, 0].astype(F32) + got_ref[0, 0].astype(F32)
    for k, send in enumerate(sends):
        send[0] = (own_ref[k + 1, 0].astype(F32) + got_ref[k + 1, 0].astype(F32)).astype(BF16)


def after_core(own, got):
    rows = own.shape[2]

    def at(y):
        return (0, y, 0, 0)

    def to(y):
        return (y, 0, 0)

    shape, block = (4, rows, 256), (1, rows, 256)
    keep, *sends = call(
        after_core_kernel,
        "after_core",
        (4,),
        [(own, (4, 1, rows, 256), at), (got, (4, 1, rows, 256), at)],
        [(shape, F32, block, to)] + [(shape, BF16, block, to)] * 3,
        flops=own.size,
    )
    return keep, sends


def after_x_kernel(keep_ref, one, two, three, out_ref, *sends):
    for y in range(4):
        value = keep_ref[y] + one[y].astype(F32) + two[y].astype(F32) + three[y].astype(F32)
        if y == 0:
            out_ref[...] = value
        else:
            sends[y - 1][...] = value.astype(BF16)


def after_x(keep, got):
    shape = keep.shape[1:]
    keep, *sends = call(
        after_x_kernel,
        "after_x",
        (1,),
        [whole(keep)] + [whole(g) for g in got],
        [out_whole(shape, F32)] + [out_whole(shape, BF16)] * 3,
        flops=keep.size * 3,
    )
    return keep, sends


def finish_feed_kernel(*refs):
    fc_ref, proj_ref = refs[-2:]
    for i in range(2):
        value = total_of(refs[4 * i : 4 * i + 4])
        fc_ref[i] = value[:128]
        proj_ref[i] = value[128:].T


def finish_feed(groups):
    return call(
        finish_feed_kernel,
        "finish_feed",
        (1,),
        [whole(a) for group in groups for a in group],
        [out_whole((2, 128, 256), F32), out_whole((2, 256, 128), F32)],
        flops=1 << 19,
    )


def finish_attention_kernel(*refs):
    qkv_ref, out_ref, small_ref = refs[-3:]
    for i in range(2):
        value = total_of(refs[4 * i : 4 * i + 4])
        qkv_ref[i, 0] = value[:128, 128:192]
        qkv_ref[i, 1] = value[:128, :64]
        qkv_ref[i, 2] = value[:128, 64:128]
        out_ref[i] = value[:128, 128:].T[64:]
        if i == 0:
            small_ref[...] = value[128:]


def finish_attention(groups):
    return call(
        finish_attention_kernel,
        "finish_attention",
        (1,),
        [whole(a) for group in groups for a in group],
        [
            out_whole((2, 3, 128, 64), F32),
            out_whole((2, 64, 128), F32),
            out_whole((16, 256), F32),
        ],
        flops=1 << 19,
    )


def pack_kernel(qkv_ref, wo_ref, fc_ref, proj_ref, bq_ref, bf_ref, gain_ref, shift_ref, *outs):
    early_ref, late_ref, last_ref = outs

    def attention(i):
        pieces = [qkv_ref[i, 1], qkv_ref[i, 2], qkv_ref[i, 0], wo_ref[i].T]
        return jnp.concatenate(pieces, axis=1)

    early_ref[:128] = attention(0)
    rows = []
    for i in range(2):
        none = jnp.zeros((1, 80), BF16)
        rows.append(jnp.concatenate([bq_ref[i, 0], bq_ref[i, 1], bf_ref[i], none], axis=1))
        rows += [gain_ref[i], shift_ref[i], jnp.zeros((1, 128), BF16)]
    small = jnp.concatenate([r.astype(F32) for r in rows], axis=0)
    small = jnp.concatenate([small, jnp.zeros_like(small)], axis=1)
    early_ref[128:] = small.astype(BF16)
    late_ref[:128] = fc_ref[0]
    late_ref[128:256] = proj_ref[0].T
    late_ref[256:] = attention(1)
    last_ref[:128] = fc_ref[1]
    last_ref[128:] = proj_ref[1].T


def pack(*arrays):
    return call(
        pack_kernel,
        "pack",
        (1,),
        [whole(a) for a in arrays],
        [
            out_whole((144, 256), BF16),
            out_whole((384, 256), BF16),
            out_whole((256, 256), BF16),
        ],
        vmem=56 << 20,
    )


def merge_kernel(me_ref, own_ref, other_ref, out_ref):
    for d in range(8):
        for ref, core in ((own_ref, 0), (other_ref, 1)):
            for x in range(2):
                t = (x ^ me_ref[1]) * 2 + (core ^ me_ref[2])
                out_ref[d, t] = ref[x, d ^ me_ref[0]]


def merge(me, own, other):
    return call(
        merge_kernel,
        "merge",
        (1,),
        [whole(own), whole(other)],
        [out_whole((8, 4, *own.shape[2:]), BF16)],
        prefetch=me,
    )[0]


def total_of(parts):
    value = parts[0][...].astype(F32)
    for part in parts[1:]:
        value = value + part[...].astype(F32)
    return value


def residual_kernel(p0, p1, p2, p3, x_ref, bias_ref, gain_ref, shift_ref, next_ref, norm_ref):
    value = x_ref[...].astype(F32) + total_of((p0, p1, p2, p3)) + bias_ref[0:1]
    next_ref[...] = value
    norm_ref[...] = (xhat_of(value)[0] * gain_ref[0:1] + shift_ref[0:1]).astype(BF16)


def add_and_norm(parts, values, bias, gain, shift):
    return call(
        residual_kernel,
        "add_and_norm",
        (1,),
        [whole(p) for p in parts] + [whole(values), whole(bias), whole(gain), whole(shift)],
        [out_whole((OWN, WIDTH), F32), out_whole((OWN, WIDTH), BF16)],
        flops=OWN * WIDTH * 16,
    )


def norm_back_kernel(p0, p1, p2, p3, x_ref, gain_ref, g_ref, out_ref, low_ref, sum_ref):
    grad = total_of((p0, p1, p2, p3))
    xhat, rstd = xhat_of(x_ref[...].astype(F32))
    dxhat = grad * gain_ref[0:1]
    into = dxhat - jnp.mean(dxhat, axis=-1, keepdims=True)
    into = (into - xhat * jnp.mean(dxhat * xhat, axis=-1, keepdims=True)) * rstd
    value = g_ref[...].astype(F32) + into
    out_ref[...] = value
    low = value.astype(BF16)
    low_ref[...] = low
    sum_ref[...] = jnp.zeros_like(sum_ref)
    sum_ref[0:1] = jnp.sum(grad * xhat, axis=0, keepdims=True)
    sum_ref[1:2] = jnp.sum(grad, axis=0, keepdims=True)
    sum_ref[2:3] = jnp.sum(low.astype(F32), axis=0, keepdims=True)


def norm_back(parts, values, gain, grad):
    return call(
        norm_back_kernel,
        "norm_back",
        (1,),
        [whole(p) for p in parts] + [whole(values), whole(gain), whole(grad)],
        [
            out_whole((OWN, WIDTH), F32),
            out_whole((OWN, WIDTH), BF16),
            out_whole((8, WIDTH), F32),
        ],
        flops=OWN * WIDTH * 32,
    )


def on_device(
    tokens, segments, cotangent, w_qkv, b_qv, w_out, w_fc, b_fc, w_proj, norm_gains, shifts
):
    layers = w_qkv.shape[0]
    xl, y, xh, z, core = (lax.axis_index(a) for a in ("xl", "y", "xh", "z", "c"))
    d_own = xl * 4 + y
    me = jnp.stack([d_own, xh, core]).astype(jnp.int32)
    first = xh == 0
    block = tokens.shape[0]

    def by_row(values):
        both = jnp.stack(values)
        kept = jnp.where(first, both[:, :, 0], both[:, :, 1])
        got = swap(jnp.where(first, both[:, :, 1], both[:, :, 0]), "xh", 1)
        lower, upper = jnp.where(first, kept, got), jnp.where(first, got, kept)
        return [jnp.concatenate([lower[k], upper[k]], axis=0) for k in range(len(values))]

    def by_position(value):
        lower, upper = value[:block], value[block:]
        kept = jnp.where(first, lower, upper)
        got = swap(jnp.where(first, upper, lower).astype(BF16), "xh", 1).astype(value.dtype)
        return jnp.stack([jnp.where(first, kept, got), jnp.where(first, got, kept)], axis=1)

    early, late, last = pack(w_qkv, w_out, w_fc, w_proj, b_qv, b_fc, norm_gains, shifts)
    one, three, two = (swap(early, "y", k) for k in (1, 3, 2))
    early = jnp.stack([early, one, two, three])
    early, tokens, cotangent = tied(early, tokens, cotangent)
    others = swaps_x([early] * 3)
    own_tokens, low = by_row([tokens, cotangent])
    all_tokens = over_z(own_tokens)
    others, all_tokens = tied(others, all_tokens)
    early = jnp.stack([early, *others]).reshape(2, 8, *early.shape[1:])
    early = merge(me, early, swap(early, "c", 1))
    late = lax.all_gather(late, PLANE, axis=0, tiled=False).reshape(8, 4, *late.shape)
    last = lax.all_gather(last, PLANE, axis=0, tiled=False).reshape(8, 4, *last.shape)
    attn_w = [(early, 0), (late, 2)]
    fc_w = [(late, 0), (last, 0)]
    proj_w = [(late, 1), (last, 1)]

    small_all = early[:, :, 128:, :128].reshape(8, 4, layers, 8, 128).transpose(2, 1, 3, 0, 4)
    rows = small_all[:, 0, 1:7].reshape(layers, 6, 1, WIDTH).astype(F32)
    rows = jnp.broadcast_to(rows, (layers, 6, 8, WIDTH))
    gains = [[rows[i, k] for k in range(2)] for i in range(layers)]
    shift = [[rows[i, 2 + k] for k in range(4)] for i in range(layers)]
    biases = small_all[:, :, 0].astype(F32)
    q_bias = biases[..., :8].reshape(layers, 4, HD)
    v_bias = biases[..., 8:16].reshape(layers, 4, HD)
    fc_bias = biases[..., 16:48].reshape(layers, 4, 1, 256)
    fc_bias = jnp.broadcast_to(fc_bias, (layers, 4, 8, 256))
    none = jnp.zeros_like(q_bias)
    qkvo_bias = jnp.concatenate([none, v_bias, q_bias, none], axis=2)[:, :, None]
    qkvo_bias = jnp.broadcast_to(qkvo_bias, (layers, 4, 8, 256))
    column = jnp.arange(256)
    scale = jnp.where(column < 2 * HD, 1.0, jnp.where(column < 3 * HD, 0.125, 0.0))
    scale = jnp.broadcast_to(scale.astype(F32), (8, 256))

    seg_row = jnp.where(first, segments[0], segments[1])
    position = jnp.arange(seg_row.shape[0], dtype=jnp.int32)

    def at_core(value, which):
        cut = value.reshape(2, 4, 2, block)
        cut = jnp.where(which == 0, cut[:, :, 0], cut[:, :, 1])
        for bit in (1, 2):
            turned = jnp.stack([cut[:, k ^ bit] for k in range(4)], axis=1)
            cut = jnp.where((z & bit) != 0, turned, cut)
        return cut.reshape(2, 4 * block)

    own_pos, own_seg = at_core(position, core), at_core(seg_row, core)
    par_pos, par_seg = at_core(position, 1 - core), at_core(seg_row, 1 - core)
    q_pos, q_seg = own_pos.reshape(-1, 1), own_seg.reshape(-1, 1)
    k_pos = jnp.concatenate([own_pos, par_pos], axis=1).reshape(1, -1)
    k_seg = jnp.concatenate([own_seg, par_seg], axis=1).reshape(1, -1)
    bias = jnp.where((q_seg == k_seg) & (q_pos >= k_pos), 0.0, -1e30).astype(F32)

    kept = []
    residual, normed = own_tokens, None
    for i in range(layers):
        attn_input = residual
        if i == 0:
            sources, norm = all_tokens, (gains[i][0], shift[i][0])
        else:
            sources, norm = over_z(normed), ()
        attn_rows, queries, kv = project(sources, norm, attn_w[i], qkvo_bias[i], scale)
        par = swap(kv, "c", 1)
        if i == 0:
            _, *cotangents = over_z(low)
        mixed, lse, *parts = attend(queries, kv, par, bias, attn_w[i])
        if i == 0:
            parts, cotangents[1] = tied(parts, cotangents[1])
        else:
            parts, cotangents = tied(parts, cotangents)
        residual, normed = add_and_norm(
            exchanged(parts), residual, shift[i][2], gains[i][1], shift[i][1]
        )
        mlp_input = residual
        mlp_rows, pre, hidden, *parts = feed(over_z(normed), fc_w[i], proj_w[i], fc_bias[i])
        after = min(i + 1, layers - 1)
        if i == layers - 1:
            last_parts = exchanged(parts)
        else:
            residual, normed = add_and_norm(
                exchanged(parts), residual, shift[i][3], gains[after][0], shift[after][0]
            )
        kept.append(
            (attn_input, attn_rows, queries, kv, par, mixed, lse, mlp_input, mlp_rows, pre, hidden)
        )
    gradient = low
    sums = jnp.sum(low.astype(F32), axis=0, keepdims=True)
    last_sums = jnp.concatenate([jnp.zeros((2, WIDTH), F32), sums, jnp.zeros((5, WIDTH), F32)])
    feed_shards, attn_shards = [None] * layers, [None] * layers
    small_sums = [None] * layers
    attn_x = None
    for i in reversed(range(layers)):
        (attn_input, attn_rows, queries, kv, par, mixed, lse, mlp_input, mlp_rows, pre, hidden) = (
            kept[i]
        )
        if i == layers - 1:
            sources = (low, *cotangents)
        else:
            got = swaps_x(attn_x[1])
            sources, got = tied(over_z(low), got)
            done = after_x(attn_x[0], got)
            attn_shards[i + 1] = (done[0], *swaps_y(done[1]))
        grad_rows, d_pre, fc_sum, *parts = feed_back(sources, fc_w[i], proj_w[i], pre)
        feed_grads = weight_grads(False, me, mlp_rows, d_pre, grad_rows, hidden)
        feed_x = after_core(feed_grads[0], swap(feed_grads[1], "c", 1))
        parts, feed_x = tied(exchanged(parts), feed_x)
        if i < layers - 1:
            parts, attn_shards[i + 1] = tied(parts, attn_shards[i + 1])
        gradient, low, feed_sums = norm_back(parts, mlp_input, gains[i][1], gradient)
        got = swaps_x(feed_x[1])
        grad_rows, dq, own_dkv, other_dkv = attend_back(
            over_z(low), attn_w[i], queries, kv, par, bias, lse
        )
        other_dkv, got, last_parts = tied(other_dkv, got, last_parts)
        if i == layers - 1:
            last, _ = add_and_norm(last_parts, residual, shift[i][3], gains[i][0], shift[i][0])
            output = by_position(last.astype(BF16))
        got_dkv = swap(other_dkv, "c", 1)
        done = after_x(feed_x[0], got)
        feed_shards[i] = (done[0], *swaps_y(done[1]))
        d_qkvo, qkvo_sum, *parts = rejoin(
            own_dkv, got_dkv, dq, attn_w[i], all_tokens if i == 0 else ()
        )
        small_sums[i] = [fc_sum, qkvo_sum, feed_sums]
        if i > 0:
            attn_grads = weight_grads(True, me, attn_rows, d_qkvo, grad_rows, mixed)
            attn_x = after_core(attn_grads[0], swap(attn_grads[1], "c", 1))
            parts, attn_x, feed_shards[i] = tied(exchanged(parts), attn_x, feed_shards[i])
            gradient, low, sums = norm_back(parts, attn_input, gains[i][0], gradient)
            small_sums[i].append(sums)
        else:
            small_sums[i].append(parts.pop())
    (fc0, qkvo0, feed0, attn0), (fc1, qkvo1, feed1, attn1) = small_sums
    extra = (fc0, fc1, qkvo0, qkvo1, attn0, feed0, attn1, feed1, last_sums)
    attn_grads = weight_grads(True, me, attn_rows, d_qkvo, grad_rows, mixed, extra)
    attn_x = after_core(attn_grads[0], swap(attn_grads[1], "c", 1))
    parts, attn_x = tied(exchanged(parts), attn_x)
    got = swaps_x(attn_x[1])
    gradient, _, _ = norm_back(parts, attn_input, gains[0][0], gradient)
    done = after_x(attn_x[0], got)
    attn_shards[0] = (done[0], *swaps_y(done[1]))
    g_tokens = by_position(gradient)
    g_w_fc, g_w_proj = finish_feed(feed_shards)
    g_w_qkv, g_w_out, mine = finish_attention(attn_shards)
    everywhere = sum(over_z(mine))
    g_b_fc = lax.dynamic_slice_in_dim(mine[:2], d_own * 32, 32, 1).reshape(layers, 1, 32)
    bias_sums = jnp.stack([mine[2:4, 128:192], mine[2:4, 64:128]], axis=1)
    g_b_qv = lax.dynamic_slice_in_dim(bias_sums, d_own * 8, 8, 2).reshape(layers, 2, 1, 8)
    vectors = everywhere[4:10].reshape(layers, 3, 2, 128)
    g_norm_gains = vectors[:, 0]
    g_shifts = jnp.concatenate([vectors[:, 1], vectors[:, 2]], axis=1)
    return (
        output,
        g_tokens,
        g_w_qkv,
        g_b_qv,
        g_w_out,
        g_w_fc,
        g_b_fc,
        g_w_proj,
        g_norm_gains,
        g_shifts,
    )


def solution(mesh):
    split = Mesh(mesh.devices.reshape(2, 4, 2, 4, 2), ("xl", "y", "xh", "z", "c"))
    dp, tensor = ("xl", "y"), ("xh", "z", "c")
    rows = P(tensor, dp, None)
    weights = (
        P(None, None, dp, tensor),
        P(None, None, tensor, dp),
        P(None, tensor, dp),
        P(None, dp, tensor),
        P(None, tensor, dp),
        P(None, tensor, dp),
        P(None, None, dp),
        P(None, None, dp),
    )
    return jax.shard_map(
        on_device,
        mesh=split,
        in_specs=(rows, P(dp, None), rows, *weights),
        out_specs=(rows, rows, *weights),
        check_vma=False,
    )
```
